32 devices in a mesh: group: 4 (over y, x), ep: 8 (over z, core).
Axes of the slice: x: 2, y: 2, z: 4, core: 2. Of those that a mesh axis runs over, the one named last changes fastest.
Arguments:
- hidden_in: bfloat16 [2, 64, 7168], P(None, 'ep'), may hold values from -6 to 6
- queries: bfloat16 [2, 64, 64, 576], P(None, 'ep', 'group'), may hold values from -60 to 60
- latent_cache: bfloat16 [2, 64, 256, 576], P(None, 'ep'), may hold values from -8 to 8
- cache_lengths: int32 [2, 64], P(None, 'ep'), may hold values from 1 to 256, as said below
- expert_ids: int32 [2, 64, 4], P(None, 'ep'), may hold values from 0 to 3, all different within a row; in each aligned block of 8 rows (0 to 7, 8 to 15, ..., all dimensions but the last counted through in order) at most 8 rows name the same one
- gate_values: float32 [2, 64, 4], P(None, 'ep'), may hold values from 0.1 to 1
- norm_gain: float32 [7168], replicated, may hold values from 0.1 to 1.9
- value_up: bfloat16 [64, 512, 128], P('group'), may hold values from -0.25 to 0.25
- out_proj: bfloat16 [8192, 7168], P('group', 'ep'), may hold values from -0.0625 to 0.0625
- gate_up: bfloat16 [8, 7168, 2, 512], P('ep', 'group'), may hold values from -0.0625 to 0.0625
- down_proj: bfloat16 [8, 512, 7168], P('ep', 'group'), may hold values from -0.1875 to 0.1875
Outputs:
- layer_out: bfloat16 [2, 64, 7168], P(None, 'ep')
The draws below stay inside these ranges and needn't reach their ends.
Inputs may be any that keep to these rules, and one draw needn't show every extreme that they name: `expert_ids`: in each micro-batch no expert is named by more than 8 of the 8 rows of one ep index, a bound that some block reaches; a row names 4 different experts. `cache_lengths`: some row of every ep index holds 256 valid positions in each micro-batch.
All inputs are finite; a program needn't handle non-finite values.
Results may differ from the reference program's by a relative error of at most 0.015.
Values may be sent and summed in bfloat16 or wider, within the bound.
A program may use at most 128 MiB of HBM per device.

```python
import math
import jax
import jax.numpy as jnp
import numpy as np
from jax import lax

D = 7168
EXP_UNITS = 1024
HEADS = 64
LATENT = 512
ROPE = 64
NOPE = 128
VDIM = 128
ROWS_DEV = 8
CACHE_LEN = 256
MB = 2
HALF = 512
KDIM = 576
NEXP = 4
TOPK = 4
ROWS = 64
CAP = 8
N_EP = 8


def cache_field(key):
    field = jax.random.normal(jax.random.fold_in(key, 101), (MB, ROWS, CACHE_LEN, KDIM), jnp.float32)
    return jnp.clip(field, -8.0, 8.0)


def draw_latent_cache(key, part):
    field = cache_field(key)
    return field.astype(jnp.bfloat16)


def draw_queries(key, part):
    key = jax.random.fold_in(key, 2)
    noise = jax.random.normal(key, (MB, ROWS, HEADS, KDIM), jnp.float32)
    return jnp.clip(noise, -60.0, 60.0).astype(jnp.bfloat16)


def draw_cache_lengths(key, part):
    key = jax.random.fold_in(key, 5)
    drawn = jax.random.randint(key, (MB, ROWS), 1, CACHE_LEN + 1, dtype=jnp.int32)
    leading = (jnp.arange(ROWS, dtype=jnp.int32) % ROWS_DEV == 0)[None, :]
    return jnp.where(leading, CACHE_LEN, drawn).astype(jnp.int32)


def block_scale(stream_key, shape, cuts, smallest, largest):
    def one(position, shards_of):
        steps = jax.random.uniform(jax.random.fold_in(jax.random.fold_in(stream_key, 6), position), (shards_of,), jnp.float32, smallest / len(cuts), largest / len(cuts))
        return jnp.repeat(jnp.exp(steps), shape[position] // shards_of).reshape((-1,) + (1,) * (len(shape) - position - 1))

    gain = one(*cuts[0])
    for cut in cuts[1:]:
        gain = gain * one(*cut)
    return gain


def assign_block(stream_key, own, number, rows, number_of, top, most, lean):
    ranking = jax.random.permutation(stream_key, number_of)
    crowded, ordinary = shares(number_of, rows * top, most, lean, True), shares(number_of, rows * top, most, lean, False)
    places = jnp.arange(number_of)

    def named(sizes, rotation):
        used = int((sizes > 0).sum())
        fixed = max(1, used // 4)
        shifted = fixed + (places - fixed + rotation * (used - fixed)) % max(1, number_of - fixed)
        return jnp.zeros((number_of,), jnp.int32).at[ranking[jnp.where(places < fixed, places, shifted)]].set(jnp.asarray(sizes, jnp.int32))

    sizes = jnp.where(number % 4 == 0, named(crowded, number // 4), named(ordinary, number - number // 4 - 1))
    mixed = jax.random.permutation(jax.random.fold_in(own, 3), number_of)
    donor, receiver = mixed[0:number_of // 2 * 2:2], mixed[1:number_of // 2 * 2:2]
    margin = jnp.minimum(sizes[donor] - 1, most - sizes[receiver]) // 2
    margin = jnp.where((donor == ranking[0]) | (receiver == ranking[0]) | (sizes[receiver] == 0), 0, jnp.maximum(margin, 0))
    shifted = jax.random.randint(jax.random.fold_in(own, 4), (number_of // 2,), 0, 1 << 20) % (margin + 1)
    sizes = sizes.at[donor].add(-shifted).at[receiver].add(shifted)
    items = jnp.searchsorted(jnp.cumsum(sizes), jnp.arange(rows * top), side="right").astype(jnp.int32)
    grid = items.reshape(top, rows).T
    grid = grid[jax.random.permutation(jax.random.fold_in(own, 1), rows)]
    rotation = jax.random.randint(jax.random.fold_in(own, 2), (rows, 1), 0, top)
    return jnp.take_along_axis(grid, (jnp.arange(top)[None, :] + rotation) % top, axis=1)


def shares(amount, total, limit, skew, full):
    loads = [(1 << 20) // math.isqrt(grade ** skew) + 1 for grade in range(1, amount + 1)]
    largest = limit if full else min(limit, max(-(-total // amount), total * loads[0] // sum(loads)))
    least = 1 if total - largest >= amount - 1 else 0
    counts, surplus = [largest] + [least] * (amount - 1), total - largest - least * (amount - 1)
    while surplus > 0:
        movable = [i for i in range(1, amount) if counts[i] < largest] or [i for i in range(1, amount) if counts[i] < limit]
        pool, budget = sum([loads[i] for i in movable]), surplus
        for i in movable:
            extra = min(limit - counts[i], max(1, budget * loads[i] // pool), surplus)
            counts[i] = counts[i] + extra
            surplus = surplus - extra
    return np.array(counts)


def normal_values(rng, extent, scale, reach, pieces=(), kind=jnp.bfloat16):
    result = scale * jax.random.normal(rng, extent, jnp.float32)
    if pieces:
        result = result * block_scale(rng, extent, pieces, -0.22, 0.18)
    return jnp.clip(result, -reach, reach).astype(kind)


def setup_inputs(seed: int = 0) -> dict:
    arg_keys = jax.random.split(jax.random.key(seed), 12)
    hidden_in = normal_values(arg_keys[0], (MB, ROWS, D), 1.0, 6.0, ((1, 8),))
    queries = draw_queries(jax.random.fold_in(arg_keys[11], 71), 0)
    latent_cache = draw_latent_cache(jax.random.fold_in(arg_keys[11], 71), 0)
    cache_lengths = draw_cache_lengths(jax.random.fold_in(arg_keys[11], 71), 0)
    expert_ids_keys = jax.random.split(jax.random.fold_in(arg_keys[4], 1), MB * ROWS // ROWS_DEV)
    expert_ids_turns = jax.random.permutation(jax.random.fold_in(arg_keys[4], 3), MB * ROWS // ROWS_DEV)
    expert_ids = jax.vmap(lambda own, number: assign_block(jax.random.fold_in(arg_keys[4], 2), own, number, ROWS_DEV, NEXP, TOPK, CAP, 2))(expert_ids_keys, expert_ids_turns).reshape((MB, ROWS, TOPK))
    gate_values = jnp.clip(0.1 + 0.9 * jax.random.uniform(arg_keys[5], (MB, ROWS, TOPK), jnp.float32) ** block_scale(arg_keys[5], (MB, ROWS, TOPK), ((1, 8),), -0.2, 0.2), 0.1, 1.0)
    norm_gain = jnp.clip(1.0 + 0.18 * jax.random.normal(arg_keys[6], (D,), jnp.float32), 0.1, 1.9)
    value_up = normal_values(arg_keys[7], (HEADS, LATENT, VDIM), LATENT ** -0.5, 0.25, ((0, 4),))
    out_proj = normal_values(arg_keys[8], (HEADS * VDIM, D), (HEADS * VDIM) ** -0.5, 0.0625, ((0, 4), (1, 8)))
    gate_up = normal_values(arg_keys[9], (2 * NEXP, D, 2, HALF), D ** -0.5, 0.0625, ((0, 8), (1, 4)))
    down_proj = normal_values(arg_keys[10], (2 * NEXP, HALF, D), EXP_UNITS ** -0.5, 0.1875, ((0, 8), (1, 4)))
    return dict(hidden_in=hidden_in, queries=queries, latent_cache=latent_cache, cache_lengths=cache_lengths, expert_ids=expert_ids, gate_values=gate_values, norm_gain=norm_gain, value_up=value_up, out_proj=out_proj, gate_up=gate_up, down_proj=down_proj)


def attend(queries, cache, lengths, value_up):
    row_count, head_count, key_width = queries.shape
    latent_width = value_up.shape[1]
    score_scale = 1.0 / math.sqrt(NOPE + ROPE)
    scores = jnp.einsum('rhk,rlk->rhl', queries.astype(jnp.float32), cache.astype(jnp.float32)) * score_scale
    in_range = jnp.arange(cache.shape[1], dtype=jnp.int32)[None, None, :] < lengths[:, None, None]
    masked = jnp.where(in_range, scores, -1e+30)
    peak_score = lax.optimization_barrier(jnp.max(masked, axis=2, keepdims=True))
    exponent = jnp.where(in_range, jnp.exp(masked - peak_score), 0.0)
    weights = (exponent / lax.optimization_barrier(jnp.sum(exponent, axis=2, keepdims=True))).astype(jnp.bfloat16)
    latent = jnp.einsum('rhl,rlc->rhc', weights.astype(jnp.float32), cache[:, :, :latent_width].astype(jnp.float32)).astype(jnp.bfloat16)
    head_out = jnp.einsum('rhc,hcv->rhv', latent.astype(jnp.float32), value_up.astype(jnp.float32)).astype(jnp.bfloat16)
    return head_out.reshape(row_count, head_count * value_up.shape[2])

def rms_scale(residual, norm_gain):
    mean_square = lax.optimization_barrier(jnp.mean(residual * residual, axis=1, keepdims=True))
    return (residual * lax.rsqrt(mean_square + 1e-06) * norm_gain[None, :]).astype(jnp.bfloat16)

def expert_layer(normed, expert_ids, gate_values, gate_up, down_proj):
    row_count = normed.shape[0]
    bound = N_EP * CAP

    def one_expert(carry, expert):
        chosen = expert_ids == expert
        coefficient = lax.optimization_barrier(jnp.sum(jnp.where(chosen, gate_values, 0.0), axis=1))
        routed = jnp.any(chosen, axis=1)
        index = jnp.nonzero(routed, size=bound, fill_value=0)[0].astype(jnp.int32)
        live = jnp.arange(bound, dtype=jnp.int32) < jnp.sum(routed.astype(jnp.int32))
        rows_in = normed[index]
        first_half = (expert * 2).astype(jnp.int32)
        pair = lax.dynamic_slice_in_dim(gate_up, first_half, 2, 0)
        gate_matrix = jnp.concatenate([pair[0, :, 0, :], pair[1, :, 0, :]], axis=1)
        up_matrix = jnp.concatenate([pair[0, :, 1, :], pair[1, :, 1, :]], axis=1)
        down_matrix = lax.dynamic_slice_in_dim(down_proj, first_half, 2, 0).reshape(EXP_UNITS, D)
        pre_gate = jnp.dot(rows_in, gate_matrix, preferred_element_type=jnp.float32)
        pre_up = jnp.dot(rows_in, up_matrix, preferred_element_type=jnp.float32)
        activation = (jax.nn.silu(pre_gate) * pre_up).astype(jnp.bfloat16)
        expert_part = jnp.dot(activation, down_matrix, preferred_element_type=jnp.float32)
        factor = jnp.where(live, coefficient[index], 0.0)
        return (carry.at[index].add(expert_part * factor[:, None]), None)
    final_mix, unused = lax.scan(one_expert, jnp.zeros((row_count, D), jnp.float32), jnp.arange(NEXP, dtype=jnp.int32))
    return final_mix

def reference(hidden_in, queries, latent_cache, cache_lengths, expert_ids, gate_values, norm_gain, value_up, out_proj, gate_up, down_proj):
    results = []
    for micro in range(MB):
        head_values = attend(queries[micro], latent_cache[micro], cache_lengths[micro], value_up)
        attended = jnp.dot(head_values, out_proj, preferred_element_type=jnp.float32)
        residual = hidden_in[micro].astype(jnp.float32) + attended
        normed = rms_scale(residual, norm_gain)
        expert_out = expert_layer(normed, expert_ids[micro], gate_values[micro], gate_up, down_proj)
        results.append((residual + expert_out).astype(jnp.bfloat16))
    return jnp.stack(results)
```

```python
import functools
import math

import jax
import jax.numpy as jnp
from jax import lax
from jax.experimental import pallas as pl
from jax.experimental.pallas import tpu as pltpu
from jax.sharding import PartitionSpec as P

ROPE = 64
NOPE = 128


def attend(queries, cache, lengths, value_up):
    row_count, head_count, key_width = queries.shape
    latent_width = value_up.shape[1]
    score_scale = 1.0 / math.sqrt(NOPE + ROPE)
    scores = (
        jnp.einsum("rhk,rlk->rhl", queries, cache, preferred_element_type=jnp.float32) * score_scale
    )
    in_range = jnp.arange(cache.shape[1], dtype=jnp.int32)[None, None, :] < lengths[:, None, None]
    masked = jnp.where(in_range, scores, -1e30)
    peak_score = jnp.max(masked, axis=2, keepdims=True)
    exponent = jnp.where(in_range, jnp.exp(masked - peak_score), 0.0)
    weights = (exponent / jnp.sum(exponent, axis=2, keepdims=True)).astype(jnp.bfloat16)
    latent = jnp.einsum(
        "rhl,rlc->rhc", weights, cache[:, :, :latent_width], preferred_element_type=jnp.float32
    ).astype(jnp.bfloat16)
    head_out = jnp.einsum(
        "rhc,hcv->rhv", latent, value_up, preferred_element_type=jnp.float32
    ).astype(jnp.bfloat16)
    return head_out.reshape(row_count, head_count * value_up.shape[2])


def rms_scale(residual, norm_gain):
    mean_square = jnp.mean(residual * residual, axis=1, keepdims=True)
    return (residual * lax.rsqrt(mean_square + 1e-06) * norm_gain[None, :]).astype(jnp.bfloat16)


def routing_tables(expert_ids, gate_values, expert_count, capacity):
    row_count, top_count = expert_ids.shape
    onehot = (
        expert_ids[:, :, None] == jnp.arange(expert_count, dtype=jnp.int32)[None, None, :]
    ).astype(jnp.int32)
    flat_hot = onehot.reshape(row_count * top_count, expert_count)
    before = jnp.cumsum(flat_hot, axis=0) - flat_hot
    slot_index = jnp.sum(before * flat_hot, axis=1).reshape(row_count, top_count)
    slot_hot = (
        slot_index[:, :, None] == jnp.arange(capacity, dtype=jnp.int32)[None, None, :]
    ).astype(jnp.float32)
    chosen = onehot.astype(jnp.float32)
    select = jnp.einsum("rke,rkc->ecr", chosen, slot_hot, precision=lax.Precision.HIGHEST)
    weighted = jnp.einsum(
        "rke,rkc,rk->ecr", chosen, slot_hot, gate_values, precision=lax.Precision.HIGHEST
    )
    return (select.astype(jnp.bfloat16), weighted)


def pack_rows(select, features):
    packed = jnp.einsum("ecr,rd->ecd", select, features, preferred_element_type=jnp.float32).astype(
        jnp.bfloat16
    )
    return jnp.repeat(packed, 2, axis=0)


def local(
    hidden_in,
    queries,
    latent_cache,
    cache_lengths,
    expert_ids,
    gate_values,
    norm_gain,
    value_up,
    out_proj,
    gate_up,
    down_proj,
):
    feature_count = hidden_in.shape[2]
    expert_count = lax.axis_size("ep") // 2
    row_local = hidden_in.shape[1]
    top_count = expert_ids.shape[2]
    capacity = min(row_local, 2 * row_local * top_count // expert_count)
    down_local = down_proj[0]
    moved = lax.all_to_all(gate_up, "group", split_axis=3, concat_axis=1, tiled=True)
    local_gate_up = moved[0].reshape(feature_count, -1)
    results = []
    for micro in range(hidden_in.shape[0]):
        head_values = attend(queries[micro], latent_cache[micro], cache_lengths[micro], value_up)
        spread = jnp.dot(
            lax.all_gather(head_values, "ep", axis=0, tiled=True),
            out_proj,
            preferred_element_type=jnp.float32,
        )
        own_rows = lax.all_to_all(spread, "ep", split_axis=0, concat_axis=1, tiled=True)
        attended = lax.psum(own_rows, "group")
        residual = hidden_in[micro].astype(jnp.float32) + attended
        normed = rms_scale(residual, norm_gain)
        select, weighted = routing_tables(
            expert_ids[micro], gate_values[micro], expert_count, capacity
        )
        outgoing = pack_rows(select, normed)
        received = lax.all_to_all(outgoing, "ep", split_axis=0, concat_axis=0, tiled=True)
        rollout_senders, rollout_item_count, width_in = received.shape
        rollout_pre_act = jnp.dot(
            received.reshape(rollout_senders * rollout_item_count, width_in),
            local_gate_up,
            preferred_element_type=jnp.float32,
        )
        pre_act = rollout_pre_act.reshape(rollout_senders * rollout_item_count, 2, -1)
        activation = (jax.nn.silu(pre_act[:, 0]) * pre_act[:, 1]).astype(jnp.bfloat16)
        block_part = jnp.dot(activation, down_local, preferred_element_type=jnp.float32).reshape(
            rollout_senders, rollout_item_count, feature_count
        )
        gathered = lax.all_to_all(
            block_part.astype(jnp.bfloat16), "ep", split_axis=0, concat_axis=0, tiled=True
        ).astype(block_part.dtype)
        gathered = gathered.reshape(expert_count, 2, capacity, -1)
        expert_mix = jnp.einsum("ecr,ehcd->rd", weighted, gathered, precision=lax.Precision.HIGHEST)
        expert_total = lax.psum(expert_mix.astype(jnp.bfloat16), "group").astype(jnp.float32)
        results.append((residual + expert_total).astype(jnp.bfloat16))
    return jnp.stack(results)


MESH = pl.DeviceIdType.MESH
BF = jnp.bfloat16
F32 = jnp.float32


def layer_kernel(
    ng,
    nep,
    hv_ref,
    hid_ref,
    coef_ref,
    gain_ref,
    wo_hbm,
    gu_hbm,
    dn_hbm,
    out_ref,
    wo,
    gu,
    dn,
    heads,
    hid_blk,
    coefs,
    s_own,
    s_send,
    s_rx,
    ag,
    ssq_own,
    ssq_rx,
    res,
    pre_send,
    pre_rx,
    part,
    sib_rx,
    chip_sum,
    grp_rx,
    grp_sum,
    z_rx,
    fin,
    load_sem,
    send_sem,
    heads_sem,
    hid_sem,
    coef_sem,
    s_sem,
    ag_sem,
    ssq_sem,
    res_sem,
    pre_sem,
    sib_sem,
    grp_sem,
    z_sem,
    fin_sem,
):
    g = lax.axis_index("group")
    j = lax.axis_index("ep")
    nz = nep // 2
    z = j // 2
    c = j % 2
    other = 1 - c
    sibling = (g, z * 2 + other)
    rows = hv_ref.shape[0]
    block = wo.shape[1]
    owners = nep // ng
    band = owners * rows
    slice_width = 2 * block

    loads = [
        pltpu.make_async_copy(wo_hbm, wo, load_sem.at[0]),
        pltpu.make_async_copy(gu_hbm, gu, load_sem.at[1]),
    ]
    for s in range(ng):
        loads.append(
            pltpu.make_async_copy(
                dn_hbm.at[:, pl.ds(s * slice_width, slice_width)], dn.at[s], load_sem.at[2 + s]
            )
        )
    for load in loads:
        load.start()

    barrier = pltpu.get_barrier_semaphore()
    ep_peers = [(g, (j + d) % nep) for d in range(1, nep)]
    g_peers = [((g + d) % ng, j) for d in range(1, ng)]
    for peer in ep_peers + g_peers:
        pl.semaphore_signal(barrier, inc=1, device_id=peer, device_id_type=MESH)
    pl.semaphore_wait(barrier, len(ep_peers) + len(g_peers))

    sends = []

    def remote(src, dst, recv, peer, index):
        return pltpu.make_async_remote_copy(
            src_ref=src,
            dst_ref=dst,
            send_sem=send_sem.at[index],
            recv_sem=recv,
            device_id=peer,
            device_id_type=MESH,
        )

    def send(src, dst, recv, peer):
        copy = remote(src, dst, recv, peer, len(sends))
        copy.start()
        sends.append(copy)

    def arrived(dst, recv):
        remote(dst, dst, recv, sibling, 0).wait_recv()

    heads[j] = hv_ref[...]
    for d in range(1, nz):
        send(heads.at[j], heads.at[j], heads_sem.at[j], (g, (z + d) % nz * 2 + c))
    send(heads.at[j], heads.at[j], heads_sem.at[j], sibling)
    coefs[j] = coef_ref[...]
    for peer in ep_peers:
        send(coefs.at[j], coefs.at[j], coef_sem.at[j], peer)

    hid_base = len(sends)
    is_source = j // owners == g
    hid_sends = []
    for k, peer in enumerate(ep_peers):
        start = pl.multiple_of(peer[1] * block, 128)
        hid_sends.append(
            remote(
                hid_ref.at[:, pl.ds(start, block)],
                hid_blk.at[j % owners],
                hid_sem.at[j % owners],
                peer,
                send_sem.shape[0] - nep + k,
            )
        )

    @pl.when(is_source)
    def _():
        for copy in hid_sends:
            copy.start()
        hid_blk[j % owners] = hid_ref[:, pl.ds(pl.multiple_of(j * block, 128), block)]

    for d in range(1, nz):
        slot = (z + d) % nz * 2 + c
        arrived(heads.at[slot], heads_sem.at[slot])
        send(heads.at[slot], heads.at[slot], heads_sem.at[slot], sibling)
    for d in range(nz):
        slot = (z + d) % nz * 2 + other
        arrived(heads.at[slot], heads_sem.at[slot])

    loads[0].wait()
    spread = jnp.dot(
        heads[...].reshape(nep * rows, heads.shape[2]), wo[...], preferred_element_type=F32
    )
    s_own[...] = spread.reshape(ng, band, block)
    s_send[...] = spread.astype(BF).reshape(ng, band, block)
    for peer in g_peers:
        send(s_send.at[peer[0]], s_rx.at[g], s_sem.at[g], peer)
    for i in range(owners):

        @pl.when(g * owners + i != j)
        def _(i=i):
            arrived(hid_blk.at[i], hid_sem.at[i])

    total = s_own[g] + hid_blk[...].reshape(band, block).astype(F32)
    for d in range(1, ng):
        slot = (g + d) % ng
        arrived(s_rx.at[slot], s_sem.at[slot])
        total = total + s_rx[slot].astype(F32)
    ag[z] = total.astype(BF)

    for d in range(1, nz):
        send(ag.at[z], ag.at[z], ag_sem.at[z], (g, (z + d) % nz * 2 + c))
    square = None
    for d in range(nz):
        slot = (z + d) % nz
        if d:
            arrived(ag.at[slot], ag_sem.at[slot])

        @pl.when(slot != g)
        def _(slot=slot, index=len(sends)):
            remote(ag.at[slot], res.at[c, g], res_sem.at[c, g], (slot, j), index).start()

        @pl.when(slot == g)
        def _(slot=slot):
            res[c, g] = ag[slot]

        sends.append((slot, remote(ag.at[slot], res.at[c, g], res_sem.at[c, g], (slot, j), len(sends))))
        value = ag[slot].astype(F32)
        term = jnp.sum(value * value, axis=1, keepdims=True)
        square = term if square is None else square + term
    ssq_own[...] = jnp.broadcast_to(square, ssq_own.shape)
    ssq_rx[c, g] = ssq_own[...]
    for peer in g_peers:
        send(ssq_own, ssq_rx.at[c, g], ssq_sem.at[c, g], peer)
    for d in range(ng):
        slot = (g + d) % ng
        if d:
            arrived(res.at[c, slot], res_sem.at[c, slot])
        send(res.at[c, slot], res.at[c, slot], res_sem.at[c, slot], sibling)
    for d in range(ng):
        slot = (g + d) % ng
        if d:
            arrived(ssq_rx.at[c, slot], ssq_sem.at[c, slot])
        send(ssq_rx.at[c, slot], ssq_rx.at[c, slot], ssq_sem.at[c, slot], sibling)
    for d in range(ng):
        slot = (g + d) % ng
        arrived(res.at[other, slot], res_sem.at[other, slot])
        arrived(ssq_rx.at[other, slot], ssq_sem.at[other, slot])

    mean_square = (ssq_rx[0] + ssq_rx[1]).reshape(ng * band, 128)[:, :1] / (nep * block)
    scale = lax.rsqrt(mean_square + 1e-06)
    loads[1].wait()
    pre = None
    for b in range(2):
        rows_in = res[b].reshape(ng * band, block).astype(F32)
        normed = (rows_in * scale * gain_ref[2 * g + b]).astype(BF)
        term = jnp.dot(normed, gu[pl.ds(b * block, block), :], preferred_element_type=F32)
        pre = term if pre is None else pre + term
    half = pre.shape[1] // 2
    units = half // ng
    for s in range(ng):
        pre_send[s, :, :units] = pre[:, s * units : (s + 1) * units].astype(BF)
        pre_send[s, :, units:] = pre[:, half + s * units : half + (s + 1) * units].astype(BF)
    for peer in g_peers:
        send(pre_send.at[peer[0]], pre_rx.at[g], pre_sem.at[g], peer)
    pre_sum = pre_send[g].astype(F32)
    for d in range(1, ng):
        slot = (g + d) % ng
        arrived(pre_rx.at[slot], pre_sem.at[slot])
        pre_sum = pre_sum + pre_rx[slot].astype(F32)
    activation = (jax.nn.silu(pre_sum[:, :units]) * pre_sum[:, units:]).astype(BF)
    for peer in ep_peers:
        arrived(coefs.at[peer[1]], coef_sem.at[peer[1]])
    lane = lax.broadcasted_iota(jnp.int32, (nep * rows, 128), 1)
    factor = jnp.sum(
        jnp.where(lane == z, coefs[...].reshape(nep * rows, 128), 0.0), axis=1, keepdims=True
    )
    for load in loads[2:]:
        load.wait()

    order = [(g + d) % ng for d in list(range(1, ng)) + [0]]
    for s in order:
        piece = jnp.dot(activation, dn[s], preferred_element_type=F32) * factor
        part[s] = piece.astype(BF).reshape(nz, 2, rows, slice_width)
        send(part.at[s, :, other], sib_rx.at[s], sib_sem.at[s], sibling)
    for s in order:
        arrived(sib_rx.at[s], sib_sem.at[s])
        chip_sum[s] = (part[s, :, c].astype(F32) + sib_rx[s].astype(F32)).astype(BF)
        if s is not order[-1]:
            send(chip_sum.at[s], grp_rx.at[g], grp_sem.at[g], (s, j))
    summed = chip_sum[g].astype(F32)
    for d in range(1, ng):
        slot = (g + d) % ng
        arrived(grp_rx.at[slot], grp_sem.at[slot])
        summed = summed + grp_rx[slot].astype(F32)
    grp_sum[...] = summed.astype(BF)
    for d in range(1, nz):
        pz = (z + d) % nz
        send(grp_sum.at[pz], z_rx.at[z], z_sem.at[z], (g, pz * 2 + c))
    own = grp_sum[z].astype(F32)
    for d in range(1, nz):
        slot = (z + d) % nz
        arrived(z_rx.at[slot], z_sem.at[slot])
        own = own + z_rx[slot].astype(F32)
    first = pl.multiple_of(j % owners * rows, rows)
    for b in range(2):
        residual = res[b, j // owners, pl.ds(first, rows), :].astype(F32)
        fin[g, :, b * block : (b + 1) * block] = (
            residual + own[:, b * block : (b + 1) * block]
        ).astype(BF)
    for peer in g_peers:
        send(fin.at[g], fin.at[g], fin_sem.at[g], peer)
    for d in range(1, ng):
        slot = (g + d) % ng
        arrived(fin.at[slot], fin_sem.at[slot])
    for s in range(ng):
        out_ref[:, s * slice_width : (s + 1) * slice_width] = fin[s]

    for copy in sends:
        if isinstance(copy, tuple):

            @pl.when(copy[0] != g)
            def _(copy=copy):
                copy[1].wait_send()

        else:
            copy.wait_send()

    @pl.when(is_source)
    def _():
        for copy in hid_sends:
            copy.wait_send()


def fused_layer(head_values, hidden, coefficient, gain, out_proj, gate_up, down):
    ng, nep = lax.axis_size("group"), lax.axis_size("ep")
    nz, owners = nep // 2, nep // ng
    rows, head_width = head_values.shape
    block = out_proj.shape[1]
    width, units = 2 * block, down.shape[0]
    band = owners * rows
    vmem, anywhere = pl.BlockSpec(memory_space=pltpu.VMEM), pl.BlockSpec(memory_space=pl.ANY)
    dma = pltpu.SemaphoreType.DMA
    return pl.pallas_call(
        functools.partial(layer_kernel, ng, nep),
        out_shape=jax.ShapeDtypeStruct((rows, nep * block), BF),
        in_specs=[vmem] * 4 + [anywhere] * 3,
        out_specs=vmem,
        scratch_shapes=[
            pltpu.VMEM(out_proj.shape, BF),
            pltpu.VMEM(gate_up.shape, BF),
            pltpu.VMEM((ng, units, width), BF),
            pltpu.VMEM((nep, rows, head_width), BF),
            pltpu.VMEM((owners, rows, block), BF),
            pltpu.VMEM((nep, rows, 128), F32),
            pltpu.VMEM((ng, band, block), F32),
            pltpu.VMEM((ng, band, block), BF),
            pltpu.VMEM((ng, band, block), BF),
            pltpu.VMEM((nz, band, block), BF),
            pltpu.VMEM((band, 128), F32),
            pltpu.VMEM((2, ng, band, 128), F32),
            pltpu.VMEM((2, ng, band, block), BF),
            pltpu.VMEM((ng, nep * rows, 2 * units), BF),
            pltpu.VMEM((ng, nep * rows, 2 * units), BF),
            pltpu.VMEM((ng, nz, 2, rows, width), BF),
            pltpu.VMEM((ng, nz, rows, width), BF),
            pltpu.VMEM((ng, nz, rows, width), BF),
            pltpu.VMEM((ng, nz, rows, width), BF),
            pltpu.VMEM((nz, rows, width), BF),
            pltpu.VMEM((nz, rows, width), BF),
            pltpu.VMEM((ng, rows, width), BF),
            dma((2 + ng,)),
            dma((96,)),
            dma((nep,)),
            dma((owners,)),
            dma((nep,)),
            dma((ng,)),
            dma((nz,)),
            dma((2, ng)),
            dma((2, ng)),
            dma((ng,)),
            dma((ng,)),
            dma((ng,)),
            dma((nz,)),
            dma((ng,)),
        ],
        compiler_params=pltpu.CompilerParams(
            collective_id=0, has_side_effects=True, vmem_limit_bytes=48 * 1024 * 1024
        ),
    )(head_values, hidden, coefficient, gain, out_proj, gate_up, down)


def local_dense(
    hidden_in,
    queries,
    latent_cache,
    cache_lengths,
    expert_ids,
    gate_values,
    norm_gain,
    value_up,
    out_proj,
    gate_up,
    down_proj,
):
    nep = lax.axis_size("ep")
    micro, row_local, feature_count = hidden_in.shape
    rows = micro * row_local

    def merged(array):
        return array.reshape((rows,) + array.shape[2:])

    head_values = attend(
        merged(queries), merged(latent_cache), cache_lengths.reshape(rows), value_up
    )
    named = merged(expert_ids)[:, :, None] == jnp.arange(128, dtype=jnp.int32)[None, None, :]
    coefficient = jnp.sum(jnp.where(named, merged(gate_values)[:, :, None], 0.0), axis=1)
    result = fused_layer(
        head_values,
        merged(hidden_in),
        coefficient,
        norm_gain.reshape(nep, 1, feature_count // nep),
        out_proj,
        gate_up[0].reshape(gate_up.shape[1], -1),
        down_proj[0],
    )
    return result.reshape(hidden_in.shape)


def layer(*args):
    hidden_in, expert_ids, down_proj = args[0], args[4], args[10]
    ng, nep = lax.axis_size("group"), lax.axis_size("ep")
    micro, row_local, feature_count = hidden_in.shape
    dense = (
        2 * expert_ids.shape[2] == nep
        and nep == 2 * ng
        and feature_count % (nep * 128) == 0
        and micro * row_local % 16 == 0
        and down_proj.shape[1] % 128 == 0
    )
    return local_dense(*args) if dense else local(*args)


def solution(mesh):
    return jax.shard_map(
        layer,
        mesh=mesh,
        in_specs=(
            P(None, "ep", None),
            P(None, "ep", "group", None),
            P(None, "ep", None, None),
            P(None, "ep"),
            P(None, "ep", None),
            P(None, "ep", None),
            P(),
            P("group", None, None),
            P("group", "ep"),
            P("ep", "group", None, None),
            P("ep", "group", None),
        ),
        out_specs=P(None, "ep", None),
        check_vma=False,
    )
```

```python
import functools
import math

import jax
import jax.numpy as jnp
from jax import lax
from jax.experimental import pallas as pl
from jax.experimental.pallas import tpu as pltpu
from jax.sharding import PartitionSpec as P

ROPE = 64
NOPE = 128


def attend(queries, cache, lengths, value_up):
    row_count, head_count, key_width = queries.shape
    latent_width = value_up.shape[1]
    score_scale = 1.0 / math.sqrt(NOPE + ROPE)
    scores = (
        jnp.einsum("rhk,rlk->rhl", queries, cache, preferred_element_type=jnp.float32) * score_scale
    )
    in_range = jnp.arange(cache.shape[1], dtype=jnp.int32)[None, None, :] < lengths[:, None, None]
    masked = jnp.where(in_range, scores, -1e30)
    peak_score = jnp.max(masked, axis=2, keepdims=True)
    exponent = jnp.where(in_range, jnp.exp(masked - peak_score), 0.0)
    weights = (exponent / jnp.sum(exponent, axis=2, keepdims=True)).astype(jnp.bfloat16)
    latent = jnp.einsum(
        "rhl,rlc->rhc", weights, cache[:, :, :latent_width], preferred_element_type=jnp.float32
    ).astype(jnp.bfloat16)
    head_out = jnp.einsum(
        "rhc,hcv->rhv", latent, value_up, preferred_element_type=jnp.float32
    ).astype(jnp.bfloat16)
    return head_out.reshape(row_count, head_count * value_up.shape[2])


def rms_scale(residual, norm_gain):
    mean_square = jnp.mean(residual * residual, axis=1, keepdims=True)
    return (residual * lax.rsqrt(mean_square + 1e-06) * norm_gain[None, :]).astype(jnp.bfloat16)


def routing_tables(expert_ids, gate_values, expert_count, capacity):
    row_count, top_count = expert_ids.shape
    onehot = (
        expert_ids[:, :, None] == jnp.arange(expert_count, dtype=jnp.int32)[None, None, :]
    ).astype(jnp.int32)
    flat_hot = onehot.reshape(row_count * top_count, expert_count)
    before = jnp.cumsum(flat_hot, axis=0) - flat_hot
    slot_index = jnp.sum(before * flat_hot, axis=1).reshape(row_count, top_count)
    slot_hot = (
        slot_index[:, :, None] == jnp.arange(capacity, dtype=jnp.int32)[None, None, :]
    ).astype(jnp.float32)
    chosen = onehot.astype(jnp.float32)
    select = jnp.einsum("rke,rkc->ecr", chosen, slot_hot, precision=lax.Precision.HIGHEST)
    weighted = jnp.einsum(
        "rke,rkc,rk->ecr", chosen, slot_hot, gate_values, precision=lax.Precision.HIGHEST
    )
    return (select.astype(jnp.bfloat16), weighted)


def pack_rows(select, features):
    packed = jnp.einsum("ecr,rd->ecd", select, features, preferred_element_type=jnp.float32).astype(
        jnp.bfloat16
    )
    return jnp.repeat(packed, 2, axis=0)


def local(
    hidden_in,
    queries,
    latent_cache,
    cache_lengths,
    expert_ids,
    gate_values,
    norm_gain,
    value_up,
    out_proj,
    gate_up,
    down_proj,
):
    feature_count = hidden_in.shape[2]
    expert_count = lax.axis_size("ep") // 2
    row_local = hidden_in.shape[1]
    top_count = expert_ids.shape[2]
    capacity = min(row_local, 2 * row_local * top_count // expert_count)
    down_local = down_proj[0]
    moved = lax.all_to_all(gate_up, "group", split_axis=3, concat_axis=1, tiled=True)
    local_gate_up = moved[0].reshape(feature_count, -1)
    results = []
    for micro in range(hidden_in.shape[0]):
        head_values = attend(queries[micro], latent_cache[micro], cache_lengths[micro], value_up)
        spread = jnp.dot(
            lax.all_gather(head_values, "ep", axis=0, tiled=True),
            out_proj,
            preferred_element_type=jnp.float32,
        )
        own_rows = lax.all_to_all(spread, "ep", split_axis=0, concat_axis=1, tiled=True)
        attended = lax.psum(own_rows, "group")
        residual = hidden_in[micro].astype(jnp.float32) + attended
        normed = rms_scale(residual, norm_gain)
        select, weighted = routing_tables(
            expert_ids[micro], gate_values[micro], expert_count, capacity
        )
        outgoing = pack_rows(select, normed)
        received = lax.all_to_all(outgoing, "ep", split_axis=0, concat_axis=0, tiled=True)
        rollout_senders, rollout_item_count, width_in = received.shape
        rollout_pre_act = jnp.dot(
            received.reshape(rollout_senders * rollout_item_count, width_in),
            local_gate_up,
            preferred_element_type=jnp.float32,
        )
        pre_act = rollout_pre_act.reshape(rollout_senders * rollout_item_count, 2, -1)
        activation = (jax.nn.silu(pre_act[:, 0]) * pre_act[:, 1]).astype(jnp.bfloat16)
        block_part = jnp.dot(activation, down_local, preferred_element_type=jnp.float32).reshape(
            rollout_senders, rollout_item_count, feature_count
        )
        gathered = lax.all_to_all(
            block_part.astype(jnp.bfloat16), "ep", split_axis=0, concat_axis=0, tiled=True
        ).astype(block_part.dtype)
        gathered = gathered.reshape(expert_count, 2, capacity, -1)
        expert_mix = jnp.einsum("ecr,ehcd->rd", weighted, gathered, precision=lax.Precision.HIGHEST)
        expert_total = lax.psum(expert_mix.astype(jnp.bfloat16), "group").astype(jnp.float32)
        results.append((residual + expert_total).astype(jnp.bfloat16))
    return jnp.stack(results)


MESH = pl.DeviceIdType.MESH
BF = jnp.bfloat16
F32 = jnp.float32


def attend_rows(len_ref, q_ref, cache, cache_loads, latents):
    rows, head_count = q_ref.shape[:2]
    length = cache.shape[1]
    latent_width = latents.shape[2]
    chunk = rows // len(cache_loads)
    score_scale = 1.0 / math.sqrt(NOPE + ROPE)
    position = lax.broadcasted_iota(jnp.int32, (head_count, length), 1)
    for r in range(rows):
        if r % chunk == 0:
            cache_loads[r // chunk].wait()
        keys = cache[r]
        scores = (
            lax.dot_general(
                q_ref[r], keys, (((1,), (1,)), ((), ())), preferred_element_type=F32
            )
            * score_scale
        )
        in_range = position < len_ref[r // len_ref.shape[1], r % len_ref.shape[1]]
        masked = jnp.where(in_range, scores, -1e30)
        peak_score = jnp.max(masked, axis=1, keepdims=True)
        exponent = jnp.where(in_range, jnp.exp(masked - peak_score), 0.0)
        weights = (exponent / jnp.sum(exponent, axis=1, keepdims=True)).astype(BF)
        latents[r] = jnp.dot(
            weights, keys[:, :latent_width], preferred_element_type=F32
        ).astype(BF)


def layer_kernel(
    ng,
    nep,
    len_ref,
    q_ref,
    hid_ref,
    coef_ref,
    gain_ref,
    cache_hbm,
    vu_hbm,
    wo_hbm,
    gu_hbm,
    dn_hbm,
    out_ref,
    cache,
    vu,
    wo,
    gu,
    dn,
    latents,
    heads,
    hid_blk,
    coefs,
    s_own,
    s_send,
    s_rx,
    ag,
    ssq_own,
    ssq_rx,
    res,
    pre_send,
    pre_rx,
    act,
    part,
    sib_rx,
    chip_sum,
    z_rx,
    fin,
    load_sem,
    send_sem,
    heads_sem,
    hid_sem,
    coef_sem,
    s_sem,
    ag_sem,
    ssq_sem,
    res_sem,
    pre_sem,
    dn_sem,
    act_sem,
    sib_sem,
    z_sem,
    fin_sem,
):
    g = lax.axis_index("group")
    j = lax.axis_index("ep")
    nz = nep // 2
    z = j // 2
    c = j % 2
    other = 1 - c
    sibling = (g, z * 2 + other)
    rows, head_count = q_ref.shape[:2]
    block = wo.shape[1]
    owners = nep // ng
    band = owners * rows
    slice_width = 2 * block

    chunk = rows // 4
    cache_loads = [
        pltpu.make_async_copy(
            cache_hbm.at[pl.ds(i * chunk, chunk)], cache.at[pl.ds(i * chunk, chunk)], load_sem.at[i]
        )
        for i in range(4)
    ]
    vu_load = pltpu.make_async_copy(vu_hbm, vu, load_sem.at[4])
    wo_load = pltpu.make_async_copy(wo_hbm, wo, load_sem.at[5])
    gu_load = pltpu.make_async_copy(gu_hbm, gu, load_sem.at[6])
    own_slice = pl.ds(pl.multiple_of(g * slice_width, 128), slice_width)
    dn_load = pltpu.make_async_copy(dn_hbm.at[:, own_slice], dn.at[g], load_sem.at[7])
    for load in cache_loads + [vu_load, wo_load, gu_load, dn_load]:
        load.start()

    barrier = pltpu.get_barrier_semaphore()
    ep_peers = [(g, (j + d) % nep) for d in range(1, nep)]
    g_peers = [((g + d) % ng, j) for d in range(1, ng)]
    for peer in ep_peers + g_peers:
        pl.semaphore_signal(barrier, inc=1, device_id=peer, device_id_type=MESH)
    pl.semaphore_wait(barrier, len(ep_peers) + len(g_peers))

    sends = []

    def remote(src, dst, recv, peer, index):
        return pltpu.make_async_remote_copy(
            src_ref=src,
            dst_ref=dst,
            send_sem=send_sem.at[index],
            recv_sem=recv,
            device_id=peer,
            device_id_type=MESH,
        )

    def send(src, dst, recv, peer):
        copy = remote(src, dst, recv, peer, len(sends))
        copy.start()
        sends.append(copy)

    def arrived(dst, recv):
        remote(dst, dst, recv, sibling, 0).wait_recv()

    for peer in g_peers:
        start = pl.multiple_of(peer[0] * slice_width, 128)
        send(dn_hbm.at[:, pl.ds(start, slice_width)], dn.at[g], dn_sem.at[g], peer)

    attend_rows(len_ref, q_ref, cache, cache_loads, latents)
    vu_load.wait()
    count = rows * head_count
    to = lax.broadcasted_iota(jnp.int32, (count, count), 0)
    source = lax.broadcasted_iota(jnp.int32, (count, count), 1)
    swap = jnp.where(source == to % rows * head_count + to // rows, 1.0, 0.0).astype(BF)
    by_head = jnp.dot(
        swap, latents[...].reshape(count, latents.shape[2]), preferred_element_type=F32
    ).astype(BF)
    value_width = vu.shape[2]
    for h in range(head_count):
        heads[j, :, h * value_width : (h + 1) * value_width] = jnp.dot(
            by_head[h * rows : (h + 1) * rows], vu[h], preferred_element_type=F32
        ).astype(BF)

    for d in range(1, nz):
        send(heads.at[j], heads.at[j], heads_sem.at[j], (g, (z + d) % nz * 2 + c))
    send(heads.at[j], heads.at[j], heads_sem.at[j], sibling)
    coefs[j] = coef_ref[...]
    for peer in ep_peers:
        send(coefs.at[j], coefs.at[j], coef_sem.at[j], peer)

    hid_base = len(sends)
    is_source = j // owners == g
    hid_sends = []
    for k, peer in enumerate(ep_peers):
        start = pl.multiple_of(peer[1] * block, 128)
        hid_sends.append(
            remote(
                hid_ref.at[:, pl.ds(start, block)],
                hid_blk.at[j % owners],
                hid_sem.at[j % owners],
                peer,
                send_sem.shape[0] - nep + k,
            )
        )

    @pl.when(is_source)
    def _():
        for copy in hid_sends:
            copy.start()
        hid_blk[j % owners] = hid_ref[:, pl.ds(pl.multiple_of(j * block, 128), block)]

    for d in range(1, nz):
        slot = (z + d) % nz * 2 + c
        arrived(heads.at[slot], heads_sem.at[slot])
        send(heads.at[slot], heads.at[slot], heads_sem.at[slot], sibling)
    for d in range(nz):
        slot = (z + d) % nz * 2 + other
        arrived(heads.at[slot], heads_sem.at[slot])

    wo_load.wait()
    spread = jnp.dot(
        heads[...].reshape(nep * rows, heads.shape[2]), wo[...], preferred_element_type=F32
    )
    s_own[...] = spread.reshape(ng, band, block)
    s_send[...] = spread.astype(BF).reshape(ng, band, block)
    for peer in g_peers:
        send(s_send.at[peer[0]], s_rx.at[g], s_sem.at[g], peer)
    for i in range(owners):

        @pl.when(g * owners + i != j)
        def _(i=i):
            arrived(hid_blk.at[i], hid_sem.at[i])

    total = s_own[g] + hid_blk[...].reshape(band, block).astype(F32)
    for d in range(1, ng):
        slot = (g + d) % ng
        arrived(s_rx.at[slot], s_sem.at[slot])
        total = total + s_rx[slot].astype(F32)
    ag[z] = total.astype(BF)

    for d in range(1, nz):
        send(ag.at[z], ag.at[z], ag_sem.at[z], (g, (z + d) % nz * 2 + c))
    square = None
    for d in range(nz):
        slot = (z + d) % nz
        if d:
            arrived(ag.at[slot], ag_sem.at[slot])

        @pl.when(slot != g)
        def _(slot=slot, index=len(sends)):
            remote(ag.at[slot], res.at[c, g], res_sem.at[c, g], (slot, j), index).start()

        @pl.when(slot == g)
        def _(slot=slot):
            res[c, g] = ag[slot]

        sends.append((slot, remote(ag.at[slot], res.at[c, g], res_sem.at[c, g], (slot, j), len(sends))))
        value = ag[slot].astype(F32)
        term = jnp.sum(value * value, axis=1, keepdims=True)
        square = term if square is None else square + term
    ssq_own[...] = jnp.broadcast_to(square, ssq_own.shape)
    ssq_rx[c, g] = ssq_own[...]
    for peer in g_peers:
        send(ssq_own, ssq_rx.at[c, g], ssq_sem.at[c, g], peer)
    for d in range(ng):
        slot = (g + d) % ng
        if d:
            arrived(res.at[c, slot], res_sem.at[c, slot])
        send(res.at[c, slot], res.at[c, slot], res_sem.at[c, slot], sibling)
    for d in range(ng):
        slot = (g + d) % ng
        if d:
            arrived(ssq_rx.at[c, slot], ssq_sem.at[c, slot])
        send(ssq_rx.at[c, slot], ssq_rx.at[c, slot], ssq_sem.at[c, slot], sibling)
    for d in range(ng):
        slot = (g + d) % ng
        arrived(res.at[other, slot], res_sem.at[other, slot])
        arrived(ssq_rx.at[other, slot], ssq_sem.at[other, slot])

    mean_square = (ssq_rx[0] + ssq_rx[1]).reshape(ng * band, 128)[:, :1] / (nep * block)
    scale = lax.rsqrt(mean_square + 1e-06)
    gu_load.wait()
    pre = None
    for b in range(2):
        rows_in = res[b].reshape(ng * band, block).astype(F32)
        normed = (rows_in * scale * gain_ref[2 * g + b]).astype(BF)
        term = jnp.dot(normed, gu[pl.ds(b * block, block), :], preferred_element_type=F32)
        pre = term if pre is None else pre + term
    half = pre.shape[1] // 2
    units = half // ng
    for s in range(ng):
        pre_send[s, :, :units] = pre[:, s * units : (s + 1) * units].astype(BF)
        pre_send[s, :, units:] = pre[:, half + s * units : half + (s + 1) * units].astype(BF)
    for peer in g_peers:
        send(pre_send.at[peer[0]], pre_rx.at[g], pre_sem.at[g], peer)
    pre_sum = pre_send[g].astype(F32)
    for d in range(1, ng):
        slot = (g + d) % ng
        arrived(pre_rx.at[slot], pre_sem.at[slot])
        pre_sum = pre_sum + pre_rx[slot].astype(F32)
    act[g] = (jax.nn.silu(pre_sum[:, :units]) * pre_sum[:, units:]).astype(BF)
    for peer in g_peers:
        send(act.at[g], act.at[g], act_sem.at[g], peer)
    for peer in ep_peers:
        arrived(coefs.at[peer[1]], coef_sem.at[peer[1]])
    lane = lax.broadcasted_iota(jnp.int32, (nep * rows, 128), 1)
    factor = jnp.sum(
        jnp.where(lane == z, coefs[...].reshape(nep * rows, 128), 0.0), axis=1, keepdims=True
    )
    dn_load.wait()
    for d in range(1, ng):
        slot = (g + d) % ng
        arrived(dn.at[slot], dn_sem.at[slot])
    for d in range(1, ng):
        slot = (g + d) % ng
        arrived(act.at[slot], act_sem.at[slot])
    activation = jnp.concatenate([act[s] for s in range(ng)], axis=1)

    for b in range(2):
        columns = dn[:, :, b * block : (b + 1) * block].reshape(ng * units, block)
        piece = jnp.dot(activation, columns, preferred_element_type=F32) * factor
        part[b] = piece.astype(BF).reshape(nz, 2, rows, block)
        send(part.at[b, :, other], sib_rx.at[b], sib_sem.at[b], sibling)
    for b in range(2):
        arrived(sib_rx.at[b], sib_sem.at[b])
        chip_sum[b] = (part[b, :, c].astype(F32) + sib_rx[b].astype(F32)).astype(BF)
        for d in range(1, nz):
            pz = (z + d) % nz
            send(chip_sum.at[b, pz], z_rx.at[b, z], z_sem.at[b, z], (g, pz * 2 + c))
    first = pl.multiple_of(j % owners * rows, rows)
    for b in range(2):
        own = chip_sum[b, z].astype(F32)
        for d in range(1, nz):
            slot = (z + d) % nz
            arrived(z_rx.at[b, slot], z_sem.at[b, slot])
            own = own + z_rx[b, slot].astype(F32)
        residual = res[b, j // owners, pl.ds(first, rows), :].astype(F32)
        fin[b, g] = (residual + own).astype(BF)
        for peer in g_peers:
            send(fin.at[b, g], fin.at[b, g], fin_sem.at[b, g], peer)
    for b in range(2):
        for d in range(1, ng):
            slot = (g + d) % ng
            arrived(fin.at[b, slot], fin_sem.at[b, slot])
    for s in range(ng):
        for b in range(2):
            start = (2 * s + b) * block
            out_ref[:, start : start + block] = fin[b, s]

    for copy in sends:
        if isinstance(copy, tuple):

            @pl.when(copy[0] != g)
            def _(copy=copy):
                copy[1].wait_send()

        else:
            copy.wait_send()

    @pl.when(is_source)
    def _():
        for copy in hid_sends:
            copy.wait_send()


def fused_layer(
    lengths, queries, hidden, coefficient, gain, cache, value_up, out_proj, gate_up, down
):
    ng, nep = lax.axis_size("group"), lax.axis_size("ep")
    nz, owners = nep // 2, nep // ng
    rows, head_count = queries.shape[:2]
    head_width = head_count * value_up.shape[2]
    block = out_proj.shape[1]
    width, units = 2 * block, down.shape[0]
    band = owners * rows
    vmem, anywhere = pl.BlockSpec(memory_space=pltpu.VMEM), pl.BlockSpec(memory_space=pl.ANY)
    dma = pltpu.SemaphoreType.DMA
    return pl.pallas_call(
        functools.partial(layer_kernel, ng, nep),
        out_shape=jax.ShapeDtypeStruct((rows, nep * block), BF),
        in_specs=[pl.BlockSpec(memory_space=pltpu.SMEM)] + [vmem] * 4 + [anywhere] * 5,
        out_specs=vmem,
        scratch_shapes=[
            pltpu.VMEM(cache.shape, BF),
            pltpu.VMEM(value_up.shape, BF),
            pltpu.VMEM(out_proj.shape, BF),
            pltpu.VMEM(gate_up.shape, BF),
            pltpu.VMEM((ng, units, width), BF),
            pltpu.VMEM((rows, head_count, value_up.shape[1]), BF),
            pltpu.VMEM((nep, rows, head_width), BF),
            pltpu.VMEM((owners, rows, block), BF),
            pltpu.VMEM((nep, rows, 128), F32),
            pltpu.VMEM((ng, band, block), F32),
            pltpu.VMEM((ng, band, block), BF),
            pltpu.VMEM((ng, band, block), BF),
            pltpu.VMEM((nz, band, block), BF),
            pltpu.VMEM((band, 128), F32),
            pltpu.VMEM((2, ng, band, 128), F32),
            pltpu.VMEM((2, ng, band, block), BF),
            pltpu.VMEM((ng, nep * rows, 2 * units), BF),
            pltpu.VMEM((ng, nep * rows, 2 * units), BF),
            pltpu.VMEM((ng, nep * rows, units), BF),
            pltpu.VMEM((2, nz, 2, rows, block), BF),
            pltpu.VMEM((2, nz, rows, block), BF),
            pltpu.VMEM((2, nz, rows, block), BF),
            pltpu.VMEM((2, nz, rows, block), BF),
            pltpu.VMEM((2, ng, rows, block), BF),
            dma((8,)),
            dma((96,)),
            dma((nep,)),
            dma((owners,)),
            dma((nep,)),
            dma((ng,)),
            dma((nz,)),
            dma((2, ng)),
            dma((2, ng)),
            dma((ng,)),
            dma((ng,)),
            dma((ng,)),
            dma((2,)),
            dma((2, nz)),
            dma((2, ng)),
        ],
        compiler_params=pltpu.CompilerParams(
            collective_id=0, has_side_effects=True, vmem_limit_bytes=48 * 1024 * 1024
        ),
    )(lengths, queries, hidden, coefficient, gain, cache, value_up, out_proj, gate_up, down)


def local_dense(
    hidden_in,
    queries,
    latent_cache,
    cache_lengths,
    expert_ids,
    gate_values,
    norm_gain,
    value_up,
    out_proj,
    gate_up,
    down_proj,
):
    nep = lax.axis_size("ep")
    micro, row_local, feature_count = hidden_in.shape
    rows = micro * row_local

    def merged(array):
        return array.reshape((rows,) + array.shape[2:])

    named = merged(expert_ids)[:, :, None] == jnp.arange(128, dtype=jnp.int32)[None, None, :]
    coefficient = jnp.sum(jnp.where(named, merged(gate_values)[:, :, None], 0.0), axis=1)
    result = fused_layer(
        cache_lengths,
        merged(queries),
        merged(hidden_in),
        coefficient,
        norm_gain.reshape(nep, 1, feature_count // nep),
        merged(latent_cache),
        value_up,
        out_proj,
        gate_up[0].reshape(gate_up.shape[1], -1),
        down_proj[0],
    )
    return result.reshape(hidden_in.shape)


def layer(*args):
    hidden_in, expert_ids, down_proj = args[0], args[4], args[10]
    ng, nep = lax.axis_size("group"), lax.axis_size("ep")
    micro, row_local, feature_count = hidden_in.shape
    dense = (
        2 * expert_ids.shape[2] == nep
        and nep == 2 * ng
        and feature_count % (nep * 128) == 0
        and micro * row_local % 16 == 0
        and down_proj.shape[1] % 128 == 0
    )
    return local_dense(*args) if dense else local(*args)


def solution(mesh):
    return jax.shard_map(
        layer,
        mesh=mesh,
        in_specs=(
            P(None, "ep", None),
            P(None, "ep", "group", None),
            P(None, "ep", None, None),
            P(None, "ep"),
            P(None, "ep", None),
            P(None, "ep", None),
            P(),
            P("group", None, None),
            P("group", "ep"),
            P("ep", "group", None, None),
            P("ep", "group", None),
        ),
        out_specs=P(None, "ep", None),
        check_vma=False,
    )
```

```python
import functools
import math

import jax
import jax.numpy as jnp
from jax import lax
from jax.experimental import pallas as pl
from jax.experimental.pallas import tpu as pltpu
from jax.sharding import PartitionSpec as P

ROPE = 64
NOPE = 128


def attend(queries, cache, lengths, value_up):
    row_count, head_count, key_width = queries.shape
    latent_width = value_up.shape[1]
    score_scale = 1.0 / math.sqrt(NOPE + ROPE)
    scores = (
        jnp.einsum("rhk,rlk->rhl", queries, cache, preferred_element_type=jnp.float32) * score_scale
    )
    in_range = jnp.arange(cache.shape[1], dtype=jnp.int32)[None, None, :] < lengths[:, None, None]
    masked = jnp.where(in_range, scores, -1e30)
    peak_score = jnp.max(masked, axis=2, keepdims=True)
    exponent = jnp.where(in_range, jnp.exp(masked - peak_score), 0.0)
    weights = (exponent / jnp.sum(exponent, axis=2, keepdims=True)).astype(jnp.bfloat16)
    latent = jnp.einsum(
        "rhl,rlc->rhc", weights, cache[:, :, :latent_width], preferred_element_type=jnp.float32
    ).astype(jnp.bfloat16)
    head_out = jnp.einsum(
        "rhc,hcv->rhv", latent, value_up, preferred_element_type=jnp.float32
    ).astype(jnp.bfloat16)
    return head_out.reshape(row_count, head_count * value_up.shape[2])


def rms_scale(residual, norm_gain):
    mean_square = jnp.mean(residual * residual, axis=1, keepdims=True)
    return (residual * lax.rsqrt(mean_square + 1e-06) * norm_gain[None, :]).astype(jnp.bfloat16)


def routing_tables(expert_ids, gate_values, expert_count, capacity):
    row_count, top_count = expert_ids.shape
    onehot = (
        expert_ids[:, :, None] == jnp.arange(expert_count, dtype=jnp.int32)[None, None, :]
    ).astype(jnp.int32)
    flat_hot = onehot.reshape(row_count * top_count, expert_count)
    before = jnp.cumsum(flat_hot, axis=0) - flat_hot
    slot_index = jnp.sum(before * flat_hot, axis=1).reshape(row_count, top_count)
    slot_hot = (
        slot_index[:, :, None] == jnp.arange(capacity, dtype=jnp.int32)[None, None, :]
    ).astype(jnp.float32)
    chosen = onehot.astype(jnp.float32)
    select = jnp.einsum("rke,rkc->ecr", chosen, slot_hot, precision=lax.Precision.HIGHEST)
    weighted = jnp.einsum(
        "rke,rkc,rk->ecr", chosen, slot_hot, gate_values, precision=lax.Precision.HIGHEST
    )
    return (select.astype(jnp.bfloat16), weighted)


def pack_rows(select, features):
    packed = jnp.einsum("ecr,rd->ecd", select, features, preferred_element_type=jnp.float32).astype(
        jnp.bfloat16
    )
    return jnp.repeat(packed, 2, axis=0)


def local(
    hidden_in,
    queries,
    latent_cache,
    cache_lengths,
    expert_ids,
    gate_values,
    norm_gain,
    value_up,
    out_proj,
    gate_up,
    down_proj,
):
    feature_count = hidden_in.shape[2]
    expert_count = lax.axis_size("ep") // 2
    row_local = hidden_in.shape[1]
    top_count = expert_ids.shape[2]
    capacity = min(row_local, 2 * row_local * top_count // expert_count)
    down_local = down_proj[0]
    moved = lax.all_to_all(gate_up, "group", split_axis=3, concat_axis=1, tiled=True)
    local_gate_up = moved[0].reshape(feature_count, -1)
    results = []
    for micro in range(hidden_in.shape[0]):
        head_values = attend(queries[micro], latent_cache[micro], cache_lengths[micro], value_up)
        spread = jnp.dot(
            lax.all_gather(head_values, "ep", axis=0, tiled=True),
            out_proj,
            preferred_element_type=jnp.float32,
        )
        own_rows = lax.all_to_all(spread, "ep", split_axis=0, concat_axis=1, tiled=True)
        attended = lax.psum(own_rows, "group")
        residual = hidden_in[micro].astype(jnp.float32) + attended
        normed = rms_scale(residual, norm_gain)
        select, weighted = routing_tables(
            expert_ids[micro], gate_values[micro], expert_count, capacity
        )
        outgoing = pack_rows(select, normed)
        received = lax.all_to_all(outgoing, "ep", split_axis=0, concat_axis=0, tiled=True)
        rollout_senders, rollout_item_count, width_in = received.shape
        rollout_pre_act = jnp.dot(
            received.reshape(rollout_senders * rollout_item_count, width_in),
            local_gate_up,
            preferred_element_type=jnp.float32,
        )
        pre_act = rollout_pre_act.reshape(rollout_senders * rollout_item_count, 2, -1)
        activation = (jax.nn.silu(pre_act[:, 0]) * pre_act[:, 1]).astype(jnp.bfloat16)
        block_part = jnp.dot(activation, down_local, preferred_element_type=jnp.float32).reshape(
            rollout_senders, rollout_item_count, feature_count
        )
        gathered = lax.all_to_all(
            block_part.astype(jnp.bfloat16), "ep", split_axis=0, concat_axis=0, tiled=True
        ).astype(block_part.dtype)
        gathered = gathered.reshape(expert_count, 2, capacity, -1)
        expert_mix = jnp.einsum("ecr,ehcd->rd", weighted, gathered, precision=lax.Precision.HIGHEST)
        expert_total = lax.psum(expert_mix.astype(jnp.bfloat16), "group").astype(jnp.float32)
        results.append((residual + expert_total).astype(jnp.bfloat16))
    return jnp.stack(results)


MESH = pl.DeviceIdType.MESH
BF = jnp.bfloat16
F32 = jnp.float32


def attend_rows(len_ref, q_ref, cache, cache_loads, latent_width):
    rows, head_count = q_ref.shape[:2]
    length = cache.shape[2]
    chunk = rows // len(cache_loads)
    score_scale = 1.0 / math.sqrt(NOPE + ROPE)
    position = lax.broadcasted_iota(jnp.int32, (head_count, length), 1)
    masked = []
    for r in range(rows):
        if r % chunk == 0:
            cache_loads[r // chunk].wait()
        scores = jnp.dot(q_ref[r], cache[r], preferred_element_type=F32) * score_scale
        in_range = position < len_ref[r // len_ref.shape[1], r % len_ref.shape[1]]
        masked.append(jnp.where(in_range, scores, -1e30))
    masked = jnp.concatenate(masked, axis=0)
    exponent = jnp.exp(masked - jnp.max(masked, axis=1, keepdims=True))
    weights = (exponent / jnp.sum(exponent, axis=1, keepdims=True)).astype(BF)
    latents = [
        lax.dot_general(
            weights[r * head_count : (r + 1) * head_count],
            cache[r, :latent_width, :],
            (((1,), (1,)), ((), ())),
            preferred_element_type=F32,
        ).astype(BF)
        for r in range(rows)
    ]
    return jnp.concatenate(latents, axis=0)


def layer_kernel(
    ng,
    nep,
    len_ref,
    q_ref,
    hid_ref,
    id_ref,
    gate_ref,
    gain_ref,
    cache_hbm,
    vu_hbm,
    wo_hbm,
    gu_hbm,
    dn_hbm,
    out_ref,
    cache,
    vu,
    wo,
    gu,
    dn,
    heads,
    hid_blk,
    coefs,
    s_own,
    s_send,
    s_rx,
    ag,
    ssq_own,
    ssq_rx,
    res,
    pre_send,
    pre_rx,
    act,
    part,
    sib_rx,
    chip_sum,
    z_rx,
    fin,
    load_sem,
    send_sem,
    heads_sem,
    hid_sem,
    coef_sem,
    s_sem,
    ag_sem,
    ssq_sem,
    res_sem,
    pre_sem,
    dn_sem,
    act_sem,
    sib_sem,
    z_sem,
    fin_sem,
):
    g = lax.axis_index("group")
    j = lax.axis_index("ep")
    nz = nep // 2
    z = j // 2
    c = j % 2
    other = 1 - c
    sibling = (g, z * 2 + other)
    rows, head_count = q_ref.shape[:2]
    block = wo.shape[1]
    owners = nep // ng
    band = owners * rows
    slice_width = 2 * block

    chunk = rows // 2
    cache_loads = [
        pltpu.make_async_copy(
            cache_hbm.at[pl.ds(i * chunk, chunk)], cache.at[pl.ds(i * chunk, chunk)], load_sem.at[i]
        )
        for i in range(2)
    ]
    vu_load = pltpu.make_async_copy(vu_hbm, vu, load_sem.at[4])
    wo_load = pltpu.make_async_copy(wo_hbm, wo, load_sem.at[5])
    gu_loads = [
        pltpu.make_async_copy(
            gu_hbm.at[:, :, pl.ds(s * 128, 128)], gu.at[s], load_sem.at[8 + s]
        )
        for s in range(ng)
    ]
    own_slice = pl.ds(pl.multiple_of(g * slice_width, 128), slice_width)
    dn_load = pltpu.make_async_copy(dn_hbm.at[:, own_slice], dn.at[g], load_sem.at[7])
    for load in cache_loads + [vu_load, wo_load, dn_load] + gu_loads:
        load.start()

    barrier = pltpu.get_barrier_semaphore()
    ep_peers = [(g, (j + d) % nep) for d in range(1, nep)]
    g_peers = [((g + d) % ng, j) for d in range(1, ng)]
    for peer in ep_peers + g_peers:
        pl.semaphore_signal(barrier, inc=1, device_id=peer, device_id_type=MESH)
    pl.semaphore_wait(barrier, len(ep_peers) + len(g_peers))

    sends = []

    def remote(src, dst, recv, peer, index):
        return pltpu.make_async_remote_copy(
            src_ref=src,
            dst_ref=dst,
            send_sem=send_sem.at[index],
            recv_sem=recv,
            device_id=peer,
            device_id_type=MESH,
        )

    def send(src, dst, recv, peer):
        copy = remote(src, dst, recv, peer, len(sends))
        copy.start()
        sends.append(copy)

    def arrived(dst, recv):
        remote(dst, dst, recv, sibling, 0).wait_recv()

    for peer in g_peers:
        start = pl.multiple_of(peer[0] * slice_width, 128)
        send(dn_hbm.at[:, pl.ds(start, slice_width)], dn.at[g], dn_sem.at[g], peer)

    latents = attend_rows(len_ref, q_ref, cache, cache_loads, vu.shape[1])
    vu_load.wait()
    count = rows * head_count
    to = lax.broadcasted_iota(jnp.int32, (count, count), 0)
    source = lax.broadcasted_iota(jnp.int32, (count, count), 1)
    swap = jnp.where(source == to % rows * head_count + to // rows, 1.0, 0.0).astype(BF)
    by_head = jnp.dot(swap, latents, preferred_element_type=F32).astype(BF)
    value_width = vu.shape[2]
    for h in range(head_count):
        heads[j, :, h * value_width : (h + 1) * value_width] = jnp.dot(
            by_head[h * rows : (h + 1) * rows], vu[h], preferred_element_type=F32
        ).astype(BF)

    for d in range(1, nz):
        send(heads.at[j], heads.at[j], heads_sem.at[j], (g, (z + d) % nz * 2 + c))
    send(heads.at[j], heads.at[j], heads_sem.at[j], sibling)
    lane = lax.broadcasted_iota(jnp.int32, (1, 128), 1)
    micro, top_count, row_local = id_ref.shape
    for r in range(rows):
        row = jnp.zeros((1, 128), F32)
        for k in range(top_count):
            m, i = r // row_local, r % row_local
            row = row + jnp.where(lane == id_ref[m, k, i], gate_ref[m, k, i], 0.0)
        coefs[j, r : r + 1, :] = row
    for peer in ep_peers:
        send(coefs.at[j], coefs.at[j], coef_sem.at[j], peer)

    hid_base = len(sends)
    is_source = j // owners == g
    hid_sends = []
    for k, peer in enumerate(ep_peers):
        start = pl.multiple_of(peer[1] * block, 128)
        hid_sends.append(
            remote(
                hid_ref.at[:, pl.ds(start, block)],
                hid_blk.at[j % owners],
                hid_sem.at[j % owners],
                peer,
                send_sem.shape[0] - nep + k,
            )
        )

    @pl.when(is_source)
    def _():
        for copy in hid_sends:
            copy.start()
        hid_blk[j % owners] = hid_ref[:, pl.ds(pl.multiple_of(j * block, 128), block)]

    for d in range(1, nz):
        slot = (z + d) % nz * 2 + c
        arrived(heads.at[slot], heads_sem.at[slot])
        send(heads.at[slot], heads.at[slot], heads_sem.at[slot], sibling)
    for d in range(nz):
        slot = (z + d) % nz * 2 + other
        arrived(heads.at[slot], heads_sem.at[slot])

    wo_load.wait()
    spread = jnp.dot(
        heads[...].reshape(nep * rows, heads.shape[2]), wo[...], preferred_element_type=F32
    )
    s_own[...] = spread.reshape(ng, band, block)
    s_send[...] = spread.astype(BF).reshape(ng, band, block)
    for peer in g_peers:
        send(s_send.at[peer[0]], s_rx.at[g], s_sem.at[g], peer)
    for i in range(owners):

        @pl.when(g * owners + i != j)
        def _(i=i):
            arrived(hid_blk.at[i], hid_sem.at[i])

    total = s_own[g] + hid_blk[...].reshape(band, block).astype(F32)
    for d in range(1, ng):
        slot = (g + d) % ng
        arrived(s_rx.at[slot], s_sem.at[slot])
        total = total + s_rx[slot].astype(F32)
    ag[z] = total.astype(BF)

    for d in range(1, nz):
        send(ag.at[z], ag.at[z], ag_sem.at[z], (g, (z + d) % nz * 2 + c))
    square = None
    for d in range(nz):
        slot = (z + d) % nz
        if d:
            arrived(ag.at[slot], ag_sem.at[slot])

        @pl.when(slot != g)
        def _(slot=slot, index=len(sends)):
            remote(ag.at[slot], res.at[c, g], res_sem.at[c, g], (slot, j), index).start()

        @pl.when(slot == g)
        def _(slot=slot):
            res[c, g] = ag[slot]

        sends.append((slot, remote(ag.at[slot], res.at[c, g], res_sem.at[c, g], (slot, j), len(sends))))
        value = ag[slot].astype(F32)
        term = jnp.sum(value * value, axis=1, keepdims=True)
        square = term if square is None else square + term
    ssq_own[...] = jnp.broadcast_to(square, ssq_own.shape)
    ssq_rx[c, g] = ssq_own[...]
    for peer in g_peers:
        send(ssq_own, ssq_rx.at[c, g], ssq_sem.at[c, g], peer)
    for d in range(ng):
        slot = (g + d) % ng
        if d:
            arrived(res.at[c, slot], res_sem.at[c, slot])
        send(res.at[c, slot], res.at[c, slot], res_sem.at[c, slot], sibling)
    for d in range(ng):
        slot = (g + d) % ng
        if d:
            arrived(ssq_rx.at[c, slot], ssq_sem.at[c, slot])
        send(ssq_rx.at[c, slot], ssq_rx.at[c, slot], ssq_sem.at[c, slot], sibling)
    for d in range(ng):
        slot = (g + d) % ng
        arrived(res.at[other, slot], res_sem.at[other, slot])
        arrived(ssq_rx.at[other, slot], ssq_sem.at[other, slot])

    mean_square = (ssq_rx[0] + ssq_rx[1]).reshape(ng * band, 128)[:, :1] / (nep * block)
    scale = lax.rsqrt(mean_square + 1e-06)
    pieces = []
    for b in range(2):
        rows_in = res[b].reshape(ng * band, block).astype(F32)
        normed = (rows_in * scale * gain_ref[2 * g + b]).astype(BF)
        pieces += [normed[:, i : i + 128] for i in range(0, block, 128)]
    feature = lax.broadcasted_iota(jnp.int32, (128, 512), 0)
    place = lax.broadcasted_iota(jnp.int32, (128, 512), 1)
    wanted = jnp.where(place < 256, 2 * feature, 256 + 2 * feature + 1)
    spacing = jnp.where(place == wanted, 1.0, 0.0).astype(BF)
    spaced = jnp.dot(
        jnp.concatenate(pieces, axis=0), spacing, preferred_element_type=F32
    ).astype(BF)
    count = ng * band
    features = jnp.concatenate(
        [
            jnp.concatenate(
                [
                    spaced[i * count : (i + 1) * count, :256],
                    spaced[i * count : (i + 1) * count, 256:],
                ],
                axis=0,
            )
            for i in range(len(pieces))
        ],
        axis=1,
    )
    for load in gu_loads:
        load.wait()
    mixed = gu.reshape(ng, 2 * gu.shape[1], 128)
    units = dn.shape[1]
    for s in range(0, ng, 2):
        columns = jnp.concatenate([mixed[s], mixed[s + 1]], axis=1)
        pre = jnp.dot(features, columns, preferred_element_type=F32).astype(BF)
        for i in range(2):
            pre_send[s + i, :, :units] = pre[:count, i * 128 : (i + 1) * 128]
            pre_send[s + i, :, units:] = pre[count:, i * 128 : (i + 1) * 128]
    for peer in g_peers:
        send(pre_send.at[peer[0]], pre_rx.at[g], pre_sem.at[g], peer)
    pre_sum = pre_send[g].astype(F32)
    for d in range(1, ng):
        slot = (g + d) % ng
        arrived(pre_rx.at[slot], pre_sem.at[slot])
        pre_sum = pre_sum + pre_rx[slot].astype(F32)
    act[g] = (jax.nn.silu(pre_sum[:, :units]) * pre_sum[:, units:]).astype(BF)
    for peer in g_peers:
        send(act.at[g], act.at[g], act_sem.at[g], peer)
    for peer in ep_peers:
        arrived(coefs.at[peer[1]], coef_sem.at[peer[1]])
    lane = lax.broadcasted_iota(jnp.int32, (nep * rows, 128), 1)
    factor = jnp.sum(
        jnp.where(lane == z, coefs[...].reshape(nep * rows, 128), 0.0), axis=1, keepdims=True
    )
    dn_load.wait()
    for d in range(1, ng):
        slot = (g + d) % ng
        arrived(dn.at[slot], dn_sem.at[slot])
    for d in range(1, ng):
        slot = (g + d) % ng
        arrived(act.at[slot], act_sem.at[slot])
    activation = jnp.concatenate([act[s] for s in range(ng)], axis=1)

    for b in range(2):
        columns = dn[:, :, b * block : (b + 1) * block].reshape(ng * units, block)
        piece = jnp.dot(activation, columns, preferred_element_type=F32) * factor
        part[b] = piece.astype(BF).reshape(nz, 2, rows, block)
        send(part.at[b, :, other], sib_rx.at[b], sib_sem.at[b], sibling)
    for b in range(2):
        arrived(sib_rx.at[b], sib_sem.at[b])
        chip_sum[b] = (part[b, :, c].astype(F32) + sib_rx[b].astype(F32)).astype(BF)
        for d in range(1, nz):
            pz = (z + d) % nz
            send(chip_sum.at[b, pz], z_rx.at[b, z], z_sem.at[b, z], (g, pz * 2 + c))
    first = pl.multiple_of(j % owners * rows, rows)
    for b in range(2):
        own = chip_sum[b, z].astype(F32)
        for d in range(1, nz):
            slot = (z + d) % nz
            arrived(z_rx.at[b, slot], z_sem.at[b, slot])
            own = own + z_rx[b, slot].astype(F32)
        residual = res[b, j // owners, pl.ds(first, rows), :].astype(F32)
        fin[b, g] = (residual + own).astype(BF)
        for peer in g_peers:
            send(fin.at[b, g], fin.at[b, g], fin_sem.at[b, g], peer)
    for b in range(2):
        for d in range(1, ng):
            slot = (g + d) % ng
            arrived(fin.at[b, slot], fin_sem.at[b, slot])
    for s in range(ng):
        for b in range(2):
            start = (2 * s + b) * block
            out_ref[:, start : start + block] = fin[b, s]

    for copy in sends:
        if isinstance(copy, tuple):

            @pl.when(copy[0] != g)
            def _(copy=copy):
                copy[1].wait_send()

        else:
            copy.wait_send()

    @pl.when(is_source)
    def _():
        for copy in hid_sends:
            copy.wait_send()


def fused_layer(
    lengths, queries, hidden, ids, gates, gain, cache, value_up, out_proj, gate_up, down
):
    ng, nep = lax.axis_size("group"), lax.axis_size("ep")
    nz, owners = nep // 2, nep // ng
    rows, head_count = queries.shape[:2]
    head_width = head_count * value_up.shape[2]
    block = out_proj.shape[1]
    width, units = 2 * block, down.shape[0]
    band = owners * rows
    vmem, anywhere = pl.BlockSpec(memory_space=pltpu.VMEM), pl.BlockSpec(memory_space=pl.ANY)
    smem, dma = pl.BlockSpec(memory_space=pltpu.SMEM), pltpu.SemaphoreType.DMA
    return pl.pallas_call(
        functools.partial(layer_kernel, ng, nep),
        out_shape=jax.ShapeDtypeStruct((rows, nep * block), BF),
        in_specs=[smem, vmem, vmem, smem, smem, vmem] + [anywhere] * 5,
        out_specs=vmem,
        scratch_shapes=[
            pltpu.VMEM(cache.shape, BF),
            pltpu.VMEM(value_up.shape, BF),
            pltpu.VMEM(out_proj.shape, BF),
            pltpu.VMEM((ng, gate_up.shape[0], 2, 128), BF),
            pltpu.VMEM((ng, units, width), BF),
            pltpu.VMEM((nep, rows, head_width), BF),
            pltpu.VMEM((owners, rows, block), BF),
            pltpu.VMEM((nep, rows, 128), F32),
            pltpu.VMEM((ng, band, block), F32),
            pltpu.VMEM((ng, band, block), BF),
            pltpu.VMEM((ng, band, block), BF),
            pltpu.VMEM((nz, band, block), BF),
            pltpu.VMEM((band, 128), F32),
            pltpu.VMEM((2, ng, band, 128), F32),
            pltpu.VMEM((2, ng, band, block), BF),
            pltpu.VMEM((ng, nep * rows, 2 * units), BF),
            pltpu.VMEM((ng, nep * rows, 2 * units), BF),
            pltpu.VMEM((ng, nep * rows, units), BF),
            pltpu.VMEM((2, nz, 2, rows, block), BF),
            pltpu.VMEM((2, nz, rows, block), BF),
            pltpu.VMEM((2, nz, rows, block), BF),
            pltpu.VMEM((2, nz, rows, block), BF),
            pltpu.VMEM((2, ng, rows, block), BF),
            dma((8 + ng,)),
            dma((96,)),
            dma((nep,)),
            dma((owners,)),
            dma((nep,)),
            dma((ng,)),
            dma((nz,)),
            dma((2, ng)),
            dma((2, ng)),
            dma((ng,)),
            dma((ng,)),
            dma((ng,)),
            dma((2,)),
            dma((2, nz)),
            dma((2, ng)),
        ],
        compiler_params=pltpu.CompilerParams(
            collective_id=0, has_side_effects=True, vmem_limit_bytes=60 * 1024 * 1024
        ),
    )(lengths, queries, hidden, ids, gates, gain, cache, value_up, out_proj, gate_up, down)


def local_dense(
    hidden_in,
    queries,
    latent_cache,
    cache_lengths,
    expert_ids,
    gate_values,
    norm_gain,
    value_up,
    out_proj,
    gate_up,
    down_proj,
):
    nep = lax.axis_size("ep")
    micro, row_local, feature_count = hidden_in.shape
    rows = micro * row_local

    def merged(array):
        return array.reshape((rows,) + array.shape[2:])

    result = fused_layer(
        cache_lengths,
        merged(queries),
        merged(hidden_in),
        jnp.swapaxes(expert_ids, 1, 2),
        jnp.swapaxes(gate_values, 1, 2),
        norm_gain.reshape(nep, 1, feature_count // nep),
        jnp.swapaxes(merged(latent_cache), 1, 2),
        value_up,
        out_proj,
        gate_up[0],
        down_proj[0],
    )
    return result.reshape(hidden_in.shape)


def layer(*args):
    hidden_in, expert_ids, down_proj = args[0], args[4], args[10]
    ng, nep = lax.axis_size("group"), lax.axis_size("ep")
    micro, row_local, feature_count = hidden_in.shape
    dense = (
        2 * expert_ids.shape[2] == nep
        and nep == 2 * ng
        and feature_count % (nep * 128) == 0
        and micro * row_local % 16 == 0
        and down_proj.shape[1] == 128
        and ng % 2 == 0
    )
    return local_dense(*args) if dense else local(*args)


def solution(mesh):
    return jax.shard_map(
        layer,
        mesh=mesh,
        in_specs=(
            P(None, "ep", None),
            P(None, "ep", "group", None),
            P(None, "ep", None, None),
            P(None, "ep"),
            P(None, "ep", None),
            P(None, "ep", None),
            P(),
            P("group", None, None),
            P("group", "ep"),
            P("ep", "group", None, None),
            P("ep", "group", None),
        ),
        out_specs=P(None, "ep", None),
        check_vma=False,
    )
```

```python
import functools
import math

import jax
import jax.numpy as jnp
from jax import lax
from jax.experimental import pallas as pl
from jax.experimental.pallas import tpu as pltpu
from jax.sharding import PartitionSpec as P

ROPE = 64
NOPE = 128


def attend(queries, cache, lengths, value_up):
    row_count, head_count, key_width = queries.shape
    latent_width = value_up.shape[1]
    score_scale = 1.0 / math.sqrt(NOPE + ROPE)
    scores = (
        jnp.einsum("rhk,rlk->rhl", queries, cache, preferred_element_type=jnp.float32) * score_scale
    )
    in_range = jnp.arange(cache.shape[1], dtype=jnp.int32)[None, None, :] < lengths[:, None, None]
    masked = jnp.where(in_range, scores, -1e30)
    peak_score = jnp.max(masked, axis=2, keepdims=True)
    exponent = jnp.where(in_range, jnp.exp(masked - peak_score), 0.0)
    weights = (exponent / jnp.sum(exponent, axis=2, keepdims=True)).astype(jnp.bfloat16)
    latent = jnp.einsum(
        "rhl,rlc->rhc", weights, cache[:, :, :latent_width], preferred_element_type=jnp.float32
    ).astype(jnp.bfloat16)
    head_out = jnp.einsum(
        "rhc,hcv->rhv", latent, value_up, preferred_element_type=jnp.float32
    ).astype(jnp.bfloat16)
    return head_out.reshape(row_count, head_count * value_up.shape[2])


def rms_scale(residual, norm_gain):
    mean_square = jnp.mean(residual * residual, axis=1, keepdims=True)
    return (residual * lax.rsqrt(mean_square + 1e-06) * norm_gain[None, :]).astype(jnp.bfloat16)


def routing_tables(expert_ids, gate_values, expert_count, capacity):
    row_count, top_count = expert_ids.shape
    onehot = (
        expert_ids[:, :, None] == jnp.arange(expert_count, dtype=jnp.int32)[None, None, :]
    ).astype(jnp.int32)
    flat_hot = onehot.reshape(row_count * top_count, expert_count)
    before = jnp.cumsum(flat_hot, axis=0) - flat_hot
    slot_index = jnp.sum(before * flat_hot, axis=1).reshape(row_count, top_count)
    slot_hot = (
        slot_index[:, :, None] == jnp.arange(capacity, dtype=jnp.int32)[None, None, :]
    ).astype(jnp.float32)
    chosen = onehot.astype(jnp.float32)
    select = jnp.einsum("rke,rkc->ecr", chosen, slot_hot, precision=lax.Precision.HIGHEST)
    weighted = jnp.einsum(
        "rke,rkc,rk->ecr", chosen, slot_hot, gate_values, precision=lax.Precision.HIGHEST
    )
    return (select.astype(jnp.bfloat16), weighted)


def pack_rows(select, features):
    packed = jnp.einsum("ecr,rd->ecd", select, features, preferred_element_type=jnp.float32).astype(
        jnp.bfloat16
    )
    return jnp.repeat(packed, 2, axis=0)


def local(
    hidden_in,
    queries,
    latent_cache,
    cache_lengths,
    expert_ids,
    gate_values,
    norm_gain,
    value_up,
    out_proj,
    gate_up,
    down_proj,
):
    feature_count = hidden_in.shape[2]
    expert_count = lax.axis_size("ep") // 2
    row_local = hidden_in.shape[1]
    top_count = expert_ids.shape[2]
    capacity = min(row_local, 2 * row_local * top_count // expert_count)
    down_local = down_proj[0]
    moved = lax.all_to_all(gate_up, "group", split_axis=3, concat_axis=1, tiled=True)
    local_gate_up = moved[0].reshape(feature_count, -1)
    results = []
    for micro in range(hidden_in.shape[0]):
        head_values = attend(queries[micro], latent_cache[micro], cache_lengths[micro], value_up)
        spread = jnp.dot(
            lax.all_gather(head_values, "ep", axis=0, tiled=True),
            out_proj,
            preferred_element_type=jnp.float32,
        )
        own_rows = lax.all_to_all(spread, "ep", split_axis=0, concat_axis=1, tiled=True)
        attended = lax.psum(own_rows, "group")
        residual = hidden_in[micro].astype(jnp.float32) + attended
        normed = rms_scale(residual, norm_gain)
        select, weighted = routing_tables(
            expert_ids[micro], gate_values[micro], expert_count, capacity
        )
        outgoing = pack_rows(select, normed)
        received = lax.all_to_all(outgoing, "ep", split_axis=0, concat_axis=0, tiled=True)
        rollout_senders, rollout_item_count, width_in = received.shape
        rollout_pre_act = jnp.dot(
            received.reshape(rollout_senders * rollout_item_count, width_in),
            local_gate_up,
            preferred_element_type=jnp.float32,
        )
        pre_act = rollout_pre_act.reshape(rollout_senders * rollout_item_count, 2, -1)
        activation = (jax.nn.silu(pre_act[:, 0]) * pre_act[:, 1]).astype(jnp.bfloat16)
        block_part = jnp.dot(activation, down_local, preferred_element_type=jnp.float32).reshape(
            rollout_senders, rollout_item_count, feature_count
        )
        gathered = lax.all_to_all(
            block_part.astype(jnp.bfloat16), "ep", split_axis=0, concat_axis=0, tiled=True
        ).astype(block_part.dtype)
        gathered = gathered.reshape(expert_count, 2, capacity, -1)
        expert_mix = jnp.einsum("ecr,ehcd->rd", weighted, gathered, precision=lax.Precision.HIGHEST)
        expert_total = lax.psum(expert_mix.astype(jnp.bfloat16), "group").astype(jnp.float32)
        results.append((residual + expert_total).astype(jnp.bfloat16))
    return jnp.stack(results)


MESH = pl.DeviceIdType.MESH
BF = jnp.bfloat16
F32 = jnp.float32


def attend_rows(len_ref, q_ref, cache, cache_loads, latent_width):
    rows, head_count = q_ref.shape[:2]
    length = cache.shape[2]
    chunk = rows // len(cache_loads)
    score_scale = 1.0 / math.sqrt(NOPE + ROPE)
    position = lax.broadcasted_iota(jnp.int32, (head_count, length), 1)
    masked = []
    for r in range(rows):
        if r % chunk == 0:
            cache_loads[r // chunk].wait()
        scores = jnp.dot(q_ref[r], cache[r], preferred_element_type=F32) * score_scale
        in_range = position < len_ref[r // len_ref.shape[1], r % len_ref.shape[1]]
        masked.append(jnp.where(in_range, scores, -1e30))
    masked = jnp.concatenate(masked, axis=0)
    exponent = jnp.exp(masked - jnp.max(masked, axis=1, keepdims=True))
    weights = (exponent / jnp.sum(exponent, axis=1, keepdims=True)).astype(BF)
    latents = [
        lax.dot_general(
            weights[r * head_count : (r + 1) * head_count],
            cache[r, :latent_width, :],
            (((1,), (1,)), ((), ())),
            preferred_element_type=F32,
        ).astype(BF)
        for r in range(rows)
    ]
    return jnp.concatenate(latents, axis=0)


def layer_kernel(
    ng,
    nep,
    len_ref,
    q_ref,
    hid_ref,
    id_ref,
    gate_ref,
    gain_ref,
    cache_hbm,
    vu_hbm,
    wo_hbm,
    gu_hbm,
    dn_hbm,
    out_ref,
    cache,
    vu,
    wo,
    gu,
    dn,
    heads,
    hid_blk,
    coefs,
    s_own,
    s_send,
    s_rx,
    ag,
    ssq_own,
    ssq_rx,
    res,
    pre_send,
    pre_rx,
    act,
    part,
    sib_rx,
    chip_sum,
    z_rx,
    fin,
    load_sem,
    send_sem,
    heads_sem,
    hid_sem,
    coef_sem,
    s_sem,
    ag_sem,
    ssq_sem,
    res_sem,
    pre_sem,
    dn_sem,
    act_sem,
    sib_sem,
    z_sem,
    fin_sem,
):
    g = lax.axis_index("group")
    j = lax.axis_index("ep")
    nz = nep // 2
    z = j // 2
    c = j % 2
    other = 1 - c
    sibling = (g, z * 2 + other)
    rows, head_count = q_ref.shape[:2]
    block = wo.shape[1]
    owners = nep // ng
    units = dn.shape[1]
    slice_width = 2 * block

    chunk = rows // 2
    cache_loads = [
        pltpu.make_async_copy(
            cache_hbm.at[pl.ds(i * chunk, chunk)], cache.at[pl.ds(i * chunk, chunk)], load_sem.at[i]
        )
        for i in range(2)
    ]
    vu_load = pltpu.make_async_copy(vu_hbm, vu, load_sem.at[4])
    wo_load = pltpu.make_async_copy(wo_hbm, wo, load_sem.at[5])
    gu_loads = [
        pltpu.make_async_copy(
            gu_hbm.at[:, :, pl.ds(s * 128, 128)], gu.at[s], load_sem.at[8 + s]
        )
        for s in range(ng)
    ]
    own_slice = pl.ds(pl.multiple_of(g * slice_width, 128), slice_width)
    dn_load = pltpu.make_async_copy(dn_hbm.at[:, own_slice], dn.at[g], load_sem.at[7])
    for load in cache_loads + [vu_load, wo_load, dn_load] + gu_loads:
        load.start()

    barrier = pltpu.get_barrier_semaphore()
    ep_peers = [(g, (j + d) % nep) for d in range(1, nep)]
    g_peers = [((g + d) % ng, j) for d in range(1, ng)]
    for peer in ep_peers + g_peers:
        pl.semaphore_signal(barrier, inc=1, device_id=peer, device_id_type=MESH)
    pl.semaphore_wait(barrier, len(ep_peers) + len(g_peers))

    sends = []

    def remote(src, dst, recv, peer, index):
        return pltpu.make_async_remote_copy(
            src_ref=src,
            dst_ref=dst,
            send_sem=send_sem.at[index],
            recv_sem=recv,
            device_id=peer,
            device_id_type=MESH,
        )

    def send(src, dst, recv, peer):
        copy = remote(src, dst, recv, peer, len(sends))
        copy.start()
        sends.append(copy)

    def send_if(wanted, src, dst, recv, peer):
        copy = remote(src, dst, recv, peer, len(sends))

        @pl.when(wanted)
        def _():
            copy.start()

        sends.append((wanted, copy))

    def arrived(dst, recv):
        remote(dst, dst, recv, sibling, 0).wait_recv()

    for peer in g_peers:
        start = pl.multiple_of(peer[0] * slice_width, 128)
        send(dn_hbm.at[:, pl.ds(start, slice_width)], dn.at[g], dn_sem.at[g], peer)

    latents = attend_rows(len_ref, q_ref, cache, cache_loads, vu.shape[1])
    vu_load.wait()
    count = rows * head_count
    to = lax.broadcasted_iota(jnp.int32, (count, count), 0)
    source = lax.broadcasted_iota(jnp.int32, (count, count), 1)
    swap = jnp.where(source == to % rows * head_count + to // rows, 1.0, 0.0).astype(BF)
    by_head = jnp.dot(swap, latents, preferred_element_type=F32).astype(BF)
    value_width = vu.shape[2]
    for h in range(head_count):
        heads[j, :, h * value_width : (h + 1) * value_width] = jnp.dot(
            by_head[h * rows : (h + 1) * rows], vu[h], preferred_element_type=F32
        ).astype(BF)

    for d in range(1, nz):
        send(heads.at[j], heads.at[j], heads_sem.at[j], (g, (z + d) % nz * 2 + c))
    send(heads.at[j], heads.at[j], heads_sem.at[j], sibling)
    lane = lax.broadcasted_iota(jnp.int32, (1, 128), 1)
    micro, top_count, row_local = id_ref.shape
    for r in range(rows):
        row = jnp.zeros((1, 128), F32)
        for k in range(top_count):
            m, i = r // row_local, r % row_local
            row = row + jnp.where(lane == id_ref[m, k, i], gate_ref[m, k, i], 0.0)
        coefs[j, r : r + 1, :] = row
    for peer in ep_peers:
        send(coefs.at[j], coefs.at[j], coef_sem.at[j], peer)

    is_source = j // owners == g
    hid_sends = []
    for k, peer in enumerate(ep_peers):
        start = pl.multiple_of(peer[1] * block, 128)
        hid_sends.append(
            remote(
                hid_ref.at[:, pl.ds(start, block)],
                hid_blk.at[j % owners],
                hid_sem.at[j % owners],
                peer,
                send_sem.shape[0] - nep + k,
            )
        )

    @pl.when(is_source)
    def _():
        for copy in hid_sends:
            copy.start()
        hid_blk[j % owners] = hid_ref[:, pl.ds(pl.multiple_of(j * block, 128), block)]

    for d in range(1, nz):
        slot = (z + d) % nz * 2 + c
        arrived(heads.at[slot], heads_sem.at[slot])
        send(heads.at[slot], heads.at[slot], heads_sem.at[slot], sibling)
    count = nz * rows

    def project(h):
        @pl.when(other == h)
        def _():
            for d in range(nz):
                slot = (z + d) % nz * 2 + other
                arrived(heads.at[slot], heads_sem.at[slot])

        rows_in = jnp.concatenate([heads[2 * i + h] for i in range(nz)], axis=0)
        spread = jnp.dot(rows_in, wo[...], preferred_element_type=F32)
        s_own[h] = spread.reshape(ng, rows, block)
        s_send[h] = spread.astype(BF).reshape(ng, rows, block)
        for peer in g_peers:
            send(s_send.at[h, peer[0]], s_rx.at[h, g], s_sem.at[h, g], peer)

    def add_heads(h):
        @pl.when(g * 2 + h != j)
        def _():
            arrived(hid_blk.at[h], hid_sem.at[h])

        total = s_own[h, g] + hid_blk[h].astype(F32)
        for d in range(1, ng):
            slot = (g + d) % ng
            arrived(s_rx.at[h, slot], s_sem.at[h, slot])
            total = total + s_rx[h, slot].astype(F32)
        ag[h, z] = total.astype(BF)
        for d in range(1, nz):
            send(ag.at[h, z], ag.at[h, z], ag_sem.at[h, z], (g, (z + d) % nz * 2 + c))

    def spread_blocks(h):
        square = None
        for d in range(nz):
            slot = (z + d) % nz
            if d:
                arrived(ag.at[h, slot], ag_sem.at[h, slot])
            send_if(
                slot != g, ag.at[h, slot], res.at[h, c, g], res_sem.at[h, c, g], (slot, j)
            )

            @pl.when(slot == g)
            def _(slot=slot):
                res[h, c, g] = ag[h, slot]

            value = ag[h, slot].astype(F32)
            term = jnp.sum(value * value, axis=1, keepdims=True)
            square = term if square is None else square + term
        ssq_own[h] = jnp.broadcast_to(square, ssq_own.shape[1:])
        ssq_rx[h, c, g] = ssq_own[h]
        for peer in g_peers:
            send(ssq_own.at[h], ssq_rx.at[h, c, g], ssq_sem.at[h, c, g], peer)

    def share_blocks(h):
        for ref, sem in ((res, res_sem), (ssq_rx, ssq_sem)):
            for d in range(ng):
                slot = (g + d) % ng
                if d:
                    arrived(ref.at[h, c, slot], sem.at[h, c, slot])
                send(ref.at[h, c, slot], ref.at[h, c, slot], sem.at[h, c, slot], sibling)

    def pre_activate(h):
        for ref, sem in ((res, res_sem), (ssq_rx, ssq_sem)):
            for d in range(ng):
                slot = (g + d) % ng
                arrived(ref.at[h, other, slot], sem.at[h, other, slot])
        mean_square = (ssq_rx[h, 0] + ssq_rx[h, 1]).reshape(count, 128)[:, :1] / (nep * block)
        scale = lax.rsqrt(mean_square + 1e-06)
        pieces = []
        for b in range(2):
            rows_in = res[h, b].reshape(count, block).astype(F32)
            normed = (rows_in * scale * gain_ref[2 * g + b]).astype(BF)
            pieces += [normed[:, i : i + 128] for i in range(0, block, 128)]
        feature = lax.broadcasted_iota(jnp.int32, (128, 512), 0)
        place = lax.broadcasted_iota(jnp.int32, (128, 512), 1)
        wanted = jnp.where(place < 256, 2 * feature, 256 + 2 * feature + 1)
        spacing = jnp.where(place == wanted, 1.0, 0.0).astype(BF)
        spaced = jnp.dot(
            jnp.concatenate(pieces, axis=0), spacing, preferred_element_type=F32
        ).astype(BF)
        features = jnp.concatenate(
            [
                jnp.concatenate(
                    [
                        spaced[i * count : (i + 1) * count, :256],
                        spaced[i * count : (i + 1) * count, 256:],
                    ],
                    axis=0,
                )
                for i in range(len(pieces))
            ],
            axis=1,
        )
        mixed = gu.reshape(ng, 2 * gu.shape[1], 128)
        for s in range(0, ng, 2):
            columns = jnp.concatenate([mixed[s], mixed[s + 1]], axis=1)
            pre = jnp.dot(features, columns, preferred_element_type=F32).astype(BF)
            for i in range(2):
                pre_send[h, s + i, :, :units] = pre[:count, i * 128 : (i + 1) * 128]
                pre_send[h, s + i, :, units:] = pre[count:, i * 128 : (i + 1) * 128]
        for peer in g_peers:
            send(pre_send.at[h, peer[0]], pre_rx.at[h, g], pre_sem.at[h, g], peer)

    def activate(h):
        pre_sum = pre_send[h, g].astype(F32)
        for d in range(1, ng):
            slot = (g + d) % ng
            arrived(pre_rx.at[h, slot], pre_sem.at[h, slot])
            pre_sum = pre_sum + pre_rx[h, slot].astype(F32)
        act[h, g] = (jax.nn.silu(pre_sum[:, :units]) * pre_sum[:, units:]).astype(BF)
        for peer in g_peers:
            send(act.at[h, g], act.at[h, g], act_sem.at[h, g], peer)

    def project_down(h):
        for d in range(1, ng):
            slot = (g + d) % ng
            arrived(act.at[h, slot], act_sem.at[h, slot])
        activation = jnp.concatenate([act[h, s] for s in range(ng)], axis=1)
        lane = lax.broadcasted_iota(jnp.int32, (count, 128), 1)
        gates = jnp.concatenate([coefs[2 * i + h] for i in range(nz)], axis=0)
        factor = jnp.sum(jnp.where(lane == z, gates, 0.0), axis=1, keepdims=True)
        for b in range(2):
            columns = dn[:, :, b * block : (b + 1) * block].reshape(ng * units, block)
            piece = jnp.dot(activation, columns, preferred_element_type=F32) * factor
            part[h, b] = piece.astype(BF).reshape(nz, rows, block)
            send_if(c != h, part.at[h, b], sib_rx.at[b], sib_sem.at[b], sibling)

    def add_cores(h):
        @pl.when(c == h)
        def _():
            for b in range(2):
                arrived(sib_rx.at[b], sib_sem.at[b])
                chip_sum[b] = (part[h, b].astype(F32) + sib_rx[b].astype(F32)).astype(BF)
                for copy in z_sends[b]:
                    copy.start()

    wo_load.wait()
    for h in range(2):
        project(h)
    for h in range(2):
        add_heads(h)
    for h in range(2):
        spread_blocks(h)
    for h in range(2):
        share_blocks(h)
    for load in gu_loads:
        load.wait()
    for h in range(2):
        pre_activate(h)
    for h in range(2):
        activate(h)
    for peer in ep_peers:
        arrived(coefs.at[peer[1]], coef_sem.at[peer[1]])
    dn_load.wait()
    for d in range(1, ng):
        slot = (g + d) % ng
        arrived(dn.at[slot], dn_sem.at[slot])
    z_sends = []
    for b in range(2):
        z_sends.append([])
        for d in range(1, nz):
            pz = (z + d) % nz
            copy = remote(
                chip_sum.at[b, pz], z_rx.at[b, z], z_sem.at[b, z], (g, pz * 2 + c), len(sends)
            )
            z_sends[b].append(copy)
            sends.append(copy)
    for h in range(2):
        project_down(h)
        add_cores(h)
    for b in range(2):
        own = chip_sum[b, z].astype(F32)
        for d in range(1, nz):
            slot = (z + d) % nz
            arrived(z_rx.at[b, slot], z_sem.at[b, slot])
            own = own + z_rx[b, slot].astype(F32)
        fin[b, g] = (res[c, b, z].astype(F32) + own).astype(BF)
        for peer in g_peers:
            send(fin.at[b, g], fin.at[b, g], fin_sem.at[b, g], peer)
    for b in range(2):
        for d in range(1, ng):
            slot = (g + d) % ng
            arrived(fin.at[b, slot], fin_sem.at[b, slot])
    for s in range(ng):
        for b in range(2):
            start = (2 * s + b) * block
            out_ref[:, start : start + block] = fin[b, s]

    for copy in sends:
        if isinstance(copy, tuple):

            @pl.when(copy[0])
            def _(copy=copy):
                copy[1].wait_send()

        else:
            copy.wait_send()

    @pl.when(is_source)
    def _():
        for copy in hid_sends:
            copy.wait_send()


def fused_layer(
    lengths, queries, hidden, ids, gates, gain, cache, value_up, out_proj, gate_up, down
):
    ng, nep = lax.axis_size("group"), lax.axis_size("ep")
    nz, owners = nep // 2, nep // ng
    rows, head_count = queries.shape[:2]
    head_width = head_count * value_up.shape[2]
    block = out_proj.shape[1]
    width, units = 2 * block, down.shape[0]
    vmem, anywhere = pl.BlockSpec(memory_space=pltpu.VMEM), pl.BlockSpec(memory_space=pl.ANY)
    smem, dma = pl.BlockSpec(memory_space=pltpu.SMEM), pltpu.SemaphoreType.DMA
    return pl.pallas_call(
        functools.partial(layer_kernel, ng, nep),
        out_shape=jax.ShapeDtypeStruct((rows, nep * block), BF),
        in_specs=[smem, vmem, vmem, smem, smem, vmem] + [anywhere] * 5,
        out_specs=vmem,
        scratch_shapes=[
            pltpu.VMEM(cache.shape, BF),
            pltpu.VMEM(value_up.shape, BF),
            pltpu.VMEM(out_proj.shape, BF),
            pltpu.VMEM((ng, gate_up.shape[0], 2, 128), BF),
            pltpu.VMEM((ng, units, width), BF),
            pltpu.VMEM((nep, rows, head_width), BF),
            pltpu.VMEM((owners, rows, block), BF),
            pltpu.VMEM((nep, rows, 128), F32),
            pltpu.VMEM((2, ng, rows, block), F32),
            pltpu.VMEM((2, ng, rows, block), BF),
            pltpu.VMEM((2, ng, rows, block), BF),
            pltpu.VMEM((2, nz, rows, block), BF),
            pltpu.VMEM((2, rows, 128), F32),
            pltpu.VMEM((2, 2, ng, rows, 128), F32),
            pltpu.VMEM((2, 2, ng, rows, block), BF),
            pltpu.VMEM((2, ng, nz * rows, 2 * units), BF),
            pltpu.VMEM((2, ng, nz * rows, 2 * units), BF),
            pltpu.VMEM((2, ng, nz * rows, units), BF),
            pltpu.VMEM((2, 2, nz, rows, block), BF),
            pltpu.VMEM((2, nz, rows, block), BF),
            pltpu.VMEM((2, nz, rows, block), BF),
            pltpu.VMEM((2, nz, rows, block), BF),
            pltpu.VMEM((2, ng, rows, block), BF),
            dma((8 + ng,)),
            dma((128,)),
            dma((nep,)),
            dma((owners,)),
            dma((nep,)),
            dma((2, ng)),
            dma((2, nz)),
            dma((2, 2, ng)),
            dma((2, 2, ng)),
            dma((2, ng)),
            dma((ng,)),
            dma((2, ng)),
            dma((2,)),
            dma((2, nz)),
            dma((2, ng)),
        ],
        compiler_params=pltpu.CompilerParams(
            collective_id=0, has_side_effects=True, vmem_limit_bytes=60 * 1024 * 1024
        ),
    )(lengths, queries, hidden, ids, gates, gain, cache, value_up, out_proj, gate_up, down)


def local_dense(
    hidden_in,
    queries,
    latent_cache,
    cache_lengths,
    expert_ids,
    gate_values,
    norm_gain,
    value_up,
    out_proj,
    gate_up,
    down_proj,
):
    nep = lax.axis_size("ep")
    micro, row_local, feature_count = hidden_in.shape
    rows = micro * row_local

    def merged(array):
        return array.reshape((rows,) + array.shape[2:])

    result = fused_layer(
        cache_lengths,
        merged(queries),
        merged(hidden_in),
        jnp.swapaxes(expert_ids, 1, 2),
        jnp.swapaxes(gate_values, 1, 2),
        norm_gain.reshape(nep, 1, feature_count // nep),
        jnp.swapaxes(merged(latent_cache), 1, 2),
        value_up,
        out_proj,
        gate_up[0],
        down_proj[0],
    )
    return result.reshape(hidden_in.shape)


def layer(*args):
    hidden_in, expert_ids, down_proj = args[0], args[4], args[10]
    ng, nep = lax.axis_size("group"), lax.axis_size("ep")
    micro, row_local, feature_count = hidden_in.shape
    dense = (
        2 * expert_ids.shape[2] == nep
        and nep == 2 * ng
        and feature_count % (nep * 128) == 0
        and micro * row_local == 16
        and down_proj.shape[1] == 128
        and ng % 2 == 0
    )
    return local_dense(*args) if dense else local(*args)


def solution(mesh):
    return jax.shard_map(
        layer,
        mesh=mesh,
        in_specs=(
            P(None, "ep", None),
            P(None, "ep", "group", None),
            P(None, "ep", None, None),
            P(None, "ep"),
            P(None, "ep", None),
            P(None, "ep", None),
            P(),
            P("group", None, None),
            P("group", "ep"),
            P("ep", "group", None, None),
            P("ep", "group", None),
        ),
        out_specs=P(None, "ep", None),
        check_vma=False,
    )
```

```python
import functools
import math

import jax
import jax.numpy as jnp
from jax import lax
from jax.experimental import pallas as pl
from jax.experimental.pallas import tpu as pltpu
from jax.sharding import PartitionSpec as P

ROPE = 64
NOPE = 128


def attend(queries, cache, lengths, value_up):
    row_count, head_count, key_width = queries.shape
    latent_width = value_up.shape[1]
    score_scale = 1.0 / math.sqrt(NOPE + ROPE)
    scores = (
        jnp.einsum("rhk,rlk->rhl", queries, cache, preferred_element_type=jnp.float32) * score_scale
    )
    in_range = jnp.arange(cache.shape[1], dtype=jnp.int32)[None, None, :] < lengths[:, None, None]
    masked = jnp.where(in_range, scores, -1e30)
    peak_score = jnp.max(masked, axis=2, keepdims=True)
    exponent = jnp.where(in_range, jnp.exp(masked - peak_score), 0.0)
    weights = (exponent / jnp.sum(exponent, axis=2, keepdims=True)).astype(jnp.bfloat16)
    latent = jnp.einsum(
        "rhl,rlc->rhc", weights, cache[:, :, :latent_width], preferred_element_type=jnp.float32
    ).astype(jnp.bfloat16)
    head_out = jnp.einsum(
        "rhc,hcv->rhv", latent, value_up, preferred_element_type=jnp.float32
    ).astype(jnp.bfloat16)
    return head_out.reshape(row_count, head_count * value_up.shape[2])


def rms_scale(residual, norm_gain):
    mean_square = jnp.mean(residual * residual, axis=1, keepdims=True)
    return (residual * lax.rsqrt(mean_square + 1e-06) * norm_gain[None, :]).astype(jnp.bfloat16)


def routing_tables(expert_ids, gate_values, expert_count, capacity):
    row_count, top_count = expert_ids.shape
    onehot = (
        expert_ids[:, :, None] == jnp.arange(expert_count, dtype=jnp.int32)[None, None, :]
    ).astype(jnp.int32)
    flat_hot = onehot.reshape(row_count * top_count, expert_count)
    before = jnp.cumsum(flat_hot, axis=0) - flat_hot
    slot_index = jnp.sum(before * flat_hot, axis=1).reshape(row_count, top_count)
    slot_hot = (
        slot_index[:, :, None] == jnp.arange(capacity, dtype=jnp.int32)[None, None, :]
    ).astype(jnp.float32)
    chosen = onehot.astype(jnp.float32)
    select = jnp.einsum("rke,rkc->ecr", chosen, slot_hot, precision=lax.Precision.HIGHEST)
    weighted = jnp.einsum(
        "rke,rkc,rk->ecr", chosen, slot_hot, gate_values, precision=lax.Precision.HIGHEST
    )
    return (select.astype(jnp.bfloat16), weighted)


def pack_rows(select, features):
    packed = jnp.einsum("ecr,rd->ecd", select, features, preferred_element_type=jnp.float32).astype(
        jnp.bfloat16
    )
    return jnp.repeat(packed, 2, axis=0)


def local(
    hidden_in,
    queries,
    latent_cache,
    cache_lengths,
    expert_ids,
    gate_values,
    norm_gain,
    value_up,
    out_proj,
    gate_up,
    down_proj,
):
    feature_count = hidden_in.shape[2]
    expert_count = lax.axis_size("ep") // 2
    row_local = hidden_in.shape[1]
    top_count = expert_ids.shape[2]
    capacity = min(row_local, 2 * row_local * top_count // expert_count)
    down_local = down_proj[0]
    moved = lax.all_to_all(gate_up, "group", split_axis=3, concat_axis=1, tiled=True)
    local_gate_up = moved[0].reshape(feature_count, -1)
    results = []
    for micro in range(hidden_in.shape[0]):
        head_values = attend(queries[micro], latent_cache[micro], cache_lengths[micro], value_up)
        spread = jnp.dot(
            lax.all_gather(head_values, "ep", axis=0, tiled=True),
            out_proj,
            preferred_element_type=jnp.float32,
        )
        own_rows = lax.all_to_all(spread, "ep", split_axis=0, concat_axis=1, tiled=True)
        attended = lax.psum(own_rows, "group")
        residual = hidden_in[micro].astype(jnp.float32) + attended
        normed = rms_scale(residual, norm_gain)
        select, weighted = routing_tables(
            expert_ids[micro], gate_values[micro], expert_count, capacity
        )
        outgoing = pack_rows(select, normed)
        received = lax.all_to_all(outgoing, "ep", split_axis=0, concat_axis=0, tiled=True)
        rollout_senders, rollout_item_count, width_in = received.shape
        rollout_pre_act = jnp.dot(
            received.reshape(rollout_senders * rollout_item_count, width_in),
            local_gate_up,
            preferred_element_type=jnp.float32,
        )
        pre_act = rollout_pre_act.reshape(rollout_senders * rollout_item_count, 2, -1)
        activation = (jax.nn.silu(pre_act[:, 0]) * pre_act[:, 1]).astype(jnp.bfloat16)
        block_part = jnp.dot(activation, down_local, preferred_element_type=jnp.float32).reshape(
            rollout_senders, rollout_item_count, feature_count
        )
        gathered = lax.all_to_all(
            block_part.astype(jnp.bfloat16), "ep", split_axis=0, concat_axis=0, tiled=True
        ).astype(block_part.dtype)
        gathered = gathered.reshape(expert_count, 2, capacity, -1)
        expert_mix = jnp.einsum("ecr,ehcd->rd", weighted, gathered, precision=lax.Precision.HIGHEST)
        expert_total = lax.psum(expert_mix.astype(jnp.bfloat16), "group").astype(jnp.float32)
        results.append((residual + expert_total).astype(jnp.bfloat16))
    return jnp.stack(results)


MESH = pl.DeviceIdType.MESH
BF = jnp.bfloat16
F32 = jnp.float32


def attend_rows(len_ref, q_ref, cache, cache_loads, latent_width):
    rows, head_count = q_ref.shape[:2]
    length = cache.shape[2]
    chunk = rows // len(cache_loads)
    score_scale = 1.0 / math.sqrt(NOPE + ROPE)
    position = lax.broadcasted_iota(jnp.int32, (head_count, length), 1)
    masked = []
    for r in range(rows):
        if r % chunk == 0:
            cache_loads[r // chunk].wait()
        scores = jnp.dot(q_ref[r], cache[r], preferred_element_type=F32) * score_scale
        in_range = position < len_ref[r // len_ref.shape[1], r % len_ref.shape[1]]
        masked.append(jnp.where(in_range, scores, -1e30))
    masked = jnp.concatenate(masked, axis=0)
    exponent = jnp.exp(masked - jnp.max(masked, axis=1, keepdims=True))
    weights = (exponent / jnp.sum(exponent, axis=1, keepdims=True)).astype(BF)
    latents = [
        lax.dot_general(
            weights[r * head_count : (r + 1) * head_count],
            cache[r, :latent_width, :],
            (((1,), (1,)), ((), ())),
            preferred_element_type=F32,
        ).astype(BF)
        for r in range(rows)
    ]
    return jnp.concatenate(latents, axis=0)


def layer_kernel(
    ng,
    nep,
    len_ref,
    q_ref,
    hid_ref,
    id_ref,
    gate_ref,
    gain_ref,
    cache_hbm,
    vu_hbm,
    wo_hbm,
    gu_hbm,
    dn_hbm,
    out_ref,
    cache,
    vu,
    wo,
    gu,
    gate_up,
    dn,
    heads,
    hid_blk,
    coefs,
    s_own,
    s_send,
    s_rx,
    ag,
    ssq_own,
    ssq_rx,
    res,
    pre_send,
    pre_rx,
    act,
    part,
    sib_rx,
    chip_sum,
    z_rx,
    fin,
    load_sem,
    send_sem,
    heads_sem,
    hid_sem,
    coef_sem,
    s_sem,
    ag_sem,
    ssq_sem,
    res_sem,
    pre_sem,
    dn_sem,
    act_sem,
    sib_sem,
    z_sem,
    fin_sem,
):
    g = lax.axis_index("group")
    j = lax.axis_index("ep")
    nz = nep // 2
    z = j // 2
    c = j % 2
    other = 1 - c
    sibling = (g, z * 2 + other)
    rows, head_count = q_ref.shape[:2]
    block = wo.shape[1]
    owners = nep // ng
    units = dn.shape[1]
    slice_width = 2 * block

    chunk = rows // 2
    cache_loads = [
        pltpu.make_async_copy(
            cache_hbm.at[pl.ds(i * chunk, chunk)], cache.at[pl.ds(i * chunk, chunk)], load_sem.at[i]
        )
        for i in range(2)
    ]
    vu_load = pltpu.make_async_copy(vu_hbm, vu, load_sem.at[4])
    wo_load = pltpu.make_async_copy(wo_hbm, wo, load_sem.at[5])
    gu_loads = [
        pltpu.make_async_copy(
            gu_hbm.at[:, :, pl.ds(s * 128, 128)], gu.at[s], load_sem.at[8 + s]
        )
        for s in range(ng)
    ]
    own_slice = pl.ds(pl.multiple_of(g * slice_width, 128), slice_width)
    dn_load = pltpu.make_async_copy(dn_hbm.at[:, own_slice], dn.at[g], load_sem.at[7])
    for load in cache_loads + [vu_load, wo_load, dn_load] + gu_loads:
        load.start()

    barrier = pltpu.get_barrier_semaphore()
    ep_peers = [(g, (j + d) % nep) for d in range(1, nep)]
    g_peers = [((g + d) % ng, j) for d in range(1, ng)]
    for peer in ep_peers + g_peers:
        pl.semaphore_signal(barrier, inc=1, device_id=peer, device_id_type=MESH)
    pl.semaphore_wait(barrier, len(ep_peers) + len(g_peers))

    sends = []

    def remote(src, dst, recv, peer, index):
        return pltpu.make_async_remote_copy(
            src_ref=src,
            dst_ref=dst,
            send_sem=send_sem.at[index],
            recv_sem=recv,
            device_id=peer,
            device_id_type=MESH,
        )

    def send(src, dst, recv, peer):
        copy = remote(src, dst, recv, peer, len(sends))
        copy.start()
        sends.append(copy)

    def send_if(wanted, src, dst, recv, peer):
        copy = remote(src, dst, recv, peer, len(sends))

        @pl.when(wanted)
        def _():
            copy.start()

        sends.append((wanted, copy))

    def arrived(dst, recv):
        remote(dst, dst, recv, sibling, 0).wait_recv()

    lane = lax.broadcasted_iota(jnp.int32, (1, 128), 1)
    micro, top_count, row_local = id_ref.shape
    for r in range(rows):
        row = jnp.zeros((1, 128), F32)
        for k in range(top_count):
            m, i = r // row_local, r % row_local
            row = row + jnp.where(lane == id_ref[m, k, i], gate_ref[m, k, i], 0.0)
        coefs[j, r : r + 1, :] = row
    for peer in ep_peers:
        send(coefs.at[j], coefs.at[j], coef_sem.at[j], peer)

    is_source = j // owners == g
    hid_sends = []
    for k, peer in enumerate(ep_peers):
        start = pl.multiple_of(peer[1] * block, 128)
        hid_sends.append(
            remote(
                hid_ref.at[:, pl.ds(start, block)],
                hid_blk.at[j % owners],
                hid_sem.at[j % owners],
                peer,
                send_sem.shape[0] - nep + k,
            )
        )

    @pl.when(is_source)
    def _():
        for copy in hid_sends:
            copy.start()
        hid_blk[j % owners] = hid_ref[:, pl.ds(pl.multiple_of(j * block, 128), block)]

    for peer in g_peers:
        start = pl.multiple_of(peer[0] * slice_width, 128)
        send(dn_hbm.at[:, pl.ds(start, slice_width)], dn.at[g], dn_sem.at[g], peer)

    latents = attend_rows(len_ref, q_ref, cache, cache_loads, vu.shape[1])
    vu_load.wait()
    count = rows * head_count
    to = lax.broadcasted_iota(jnp.int32, (count, count), 0)
    source = lax.broadcasted_iota(jnp.int32, (count, count), 1)
    swap = jnp.where(source == to % rows * head_count + to // rows, 1.0, 0.0).astype(BF)
    by_head = jnp.dot(swap, latents, preferred_element_type=F32).astype(BF)
    value_width = vu.shape[2]
    for h in range(head_count):
        heads[j, :, h * value_width : (h + 1) * value_width] = jnp.dot(
            by_head[h * rows : (h + 1) * rows], vu[h], preferred_element_type=F32
        ).astype(BF)

    for d in range(1, nz):
        send(heads.at[j], heads.at[j], heads_sem.at[j], (g, (z + d) % nz * 2 + c))
    send(heads.at[j], heads.at[j], heads_sem.at[j], sibling)
    for load in gu_loads:
        load.wait()
    to = lax.broadcasted_iota(jnp.int32, (256, 256), 0)
    source = lax.broadcasted_iota(jnp.int32, (256, 256), 1)
    wanted = jnp.where(to < 128, 2 * to, 2 * (to - 128) + 1)
    order = jnp.where(source == wanted, 1.0, 0.0).astype(BF)
    mixed = gu.reshape(ng, 2 * gu.shape[1], 128)
    for t in range(gu.shape[1] // 128):
        lines = jnp.concatenate([mixed[s, t * 256 : (t + 1) * 256, :] for s in range(ng)], axis=1)
        sorted_lines = jnp.dot(order, lines, preferred_element_type=F32).astype(BF)
        for s in range(ng):
            for i in range(2):
                gate_up[t * 128 : (t + 1) * 128, s * 256 + i * 128 : s * 256 + (i + 1) * 128] = (
                    sorted_lines[i * 128 : (i + 1) * 128, s * 128 : (s + 1) * 128]
                )

    for d in range(1, nz):
        slot = (z + d) % nz * 2 + c
        arrived(heads.at[slot], heads_sem.at[slot])
        send(heads.at[slot], heads.at[slot], heads_sem.at[slot], sibling)
    count = nz * rows

    def project(h):
        @pl.when(other == h)
        def _():
            for d in range(nz):
                slot = (z + d) % nz * 2 + other
                arrived(heads.at[slot], heads_sem.at[slot])

        rows_in = jnp.concatenate([heads[2 * i + h] for i in range(nz)], axis=0)
        spread = jnp.dot(rows_in, wo[...], preferred_element_type=F32)
        s_own[h] = spread.reshape(ng, rows, block)
        s_send[h] = spread.astype(BF).reshape(ng, rows, block)
        for peer in g_peers:
            send(s_send.at[h, peer[0]], s_rx.at[h, g], s_sem.at[h, g], peer)

    def add_heads(h):
        @pl.when(g * 2 + h != j)
        def _():
            arrived(hid_blk.at[h], hid_sem.at[h])

        total = s_own[h, g] + hid_blk[h].astype(F32)
        for d in range(1, ng):
            slot = (g + d) % ng
            arrived(s_rx.at[h, slot], s_sem.at[h, slot])
            total = total + s_rx[h, slot].astype(F32)
        ag[h, z] = total.astype(BF)
        for d in range(1, nz):
            send(ag.at[h, z], ag.at[h, z], ag_sem.at[h, z], (g, (z + d) % nz * 2 + c))

    def spread_blocks(h):
        square = None
        for d in range(nz):
            slot = (z + d) % nz
            if d:
                arrived(ag.at[h, slot], ag_sem.at[h, slot])
            send_if(
                slot != g, ag.at[h, slot], res.at[h, c, g], res_sem.at[h, c, g], (slot, j)
            )

            @pl.when(slot == g)
            def _(slot=slot):
                res[h, c, g] = ag[h, slot]

            value = ag[h, slot].astype(F32)
            term = jnp.sum(value * value, axis=1, keepdims=True)
            square = term if square is None else square + term
        ssq_own[h] = jnp.broadcast_to(square, ssq_own.shape[1:])
        ssq_rx[h, c, g] = ssq_own[h]
        for peer in g_peers:
            send(ssq_own.at[h], ssq_rx.at[h, c, g], ssq_sem.at[h, c, g], peer)

    def share_blocks(h):
        for ref, sem in ((res, res_sem), (ssq_rx, ssq_sem)):
            for d in range(ng):
                slot = (g + d) % ng
                if d:
                    arrived(ref.at[h, c, slot], sem.at[h, c, slot])
                send(ref.at[h, c, slot], ref.at[h, c, slot], sem.at[h, c, slot], sibling)

    def pre_activate(h):
        for ref, sem in ((res, res_sem), (ssq_rx, ssq_sem)):
            for d in range(ng):
                slot = (g + d) % ng
                arrived(ref.at[h, other, slot], sem.at[h, other, slot])
        mean_square = (ssq_rx[h, 0] + ssq_rx[h, 1]).reshape(count, 128)[:, :1] / (nep * block)
        scale = lax.rsqrt(mean_square + 1e-06)
        pieces = []
        for b in range(2):
            rows_in = res[h, b].reshape(count, block).astype(F32)
            pieces.append((rows_in * scale * gain_ref[2 * g + b]).astype(BF))
        pre = jnp.dot(
            jnp.concatenate(pieces, axis=1), gate_up[...], preferred_element_type=F32
        ).astype(BF)
        for s in range(ng):
            pre_send[h, s] = pre[:, s * 2 * units : (s + 1) * 2 * units]
        for peer in g_peers:
            send(pre_send.at[h, peer[0]], pre_rx.at[h, g], pre_sem.at[h, g], peer)

    def activate(h):
        pre_sum = pre_send[h, g].astype(F32)
        for d in range(1, ng):
            slot = (g + d) % ng
            arrived(pre_rx.at[h, slot], pre_sem.at[h, slot])
            pre_sum = pre_sum + pre_rx[h, slot].astype(F32)
        act[h, g] = (jax.nn.silu(pre_sum[:, :units]) * pre_sum[:, units:]).astype(BF)
        for peer in g_peers:
            send(act.at[h, g], act.at[h, g], act_sem.at[h, g], peer)

    def project_down(h):
        for d in range(1, ng):
            slot = (g + d) % ng
            arrived(act.at[h, slot], act_sem.at[h, slot])
        activation = jnp.concatenate([act[h, s] for s in range(ng)], axis=1)
        lane = lax.broadcasted_iota(jnp.int32, (count, 128), 1)
        gates = jnp.concatenate([coefs[2 * i + h] for i in range(nz)], axis=0)
        factor = jnp.sum(jnp.where(lane == z, gates, 0.0), axis=1, keepdims=True)
        for b in range(2):
            columns = dn[:, :, b * block : (b + 1) * block].reshape(ng * units, block)
            piece = jnp.dot(activation, columns, preferred_element_type=F32) * factor
            part[h, b] = piece.astype(BF).reshape(nz, rows, block)
            send_if(c != h, part.at[h, b], sib_rx.at[b], sib_sem.at[b], sibling)

    def add_cores(h):
        @pl.when(c == h)
        def _():
            for b in range(2):
                arrived(sib_rx.at[b], sib_sem.at[b])
                chip_sum[b] = (part[h, b].astype(F32) + sib_rx[b].astype(F32)).astype(BF)
                for copy in z_sends[b]:
                    copy.start()

    wo_load.wait()
    for h in range(2):
        project(h)
    for h in range(2):
        add_heads(h)
    for h in range(2):
        spread_blocks(h)
    for h in range(2):
        share_blocks(h)
    for h in range(2):
        pre_activate(h)
    for h in range(2):
        activate(h)
    for peer in ep_peers:
        arrived(coefs.at[peer[1]], coef_sem.at[peer[1]])
    dn_load.wait()
    for d in range(1, ng):
        slot = (g + d) % ng
        arrived(dn.at[slot], dn_sem.at[slot])
    z_sends = []
    for b in range(2):
        z_sends.append([])
        for d in range(1, nz):
            pz = (z + d) % nz
            copy = remote(
                chip_sum.at[b, pz], z_rx.at[b, z], z_sem.at[b, z], (g, pz * 2 + c), len(sends)
            )
            z_sends[b].append(copy)
            sends.append(copy)
    for h in range(2):
        project_down(h)
        add_cores(h)
    for b in range(2):
        own = chip_sum[b, z].astype(F32)
        for d in range(1, nz):
            slot = (z + d) % nz
            arrived(z_rx.at[b, slot], z_sem.at[b, slot])
            own = own + z_rx[b, slot].astype(F32)
        fin[b, g] = (res[c, b, z].astype(F32) + own).astype(BF)
        for peer in g_peers:
            send(fin.at[b, g], fin.at[b, g], fin_sem.at[b, g], peer)
    for b in range(2):
        for d in range(1, ng):
            slot = (g + d) % ng
            arrived(fin.at[b, slot], fin_sem.at[b, slot])
    for s in range(ng):
        for b in range(2):
            start = (2 * s + b) * block
            out_ref[:, start : start + block] = fin[b, s]

    for copy in sends:
        if isinstance(copy, tuple):

            @pl.when(copy[0])
            def _(copy=copy):
                copy[1].wait_send()

        else:
            copy.wait_send()

    @pl.when(is_source)
    def _():
        for copy in hid_sends:
            copy.wait_send()


def fused_layer(
    lengths, queries, hidden, ids, gates, gain, cache, value_up, out_proj, gate_up, down
):
    ng, nep = lax.axis_size("group"), lax.axis_size("ep")
    nz, owners = nep // 2, nep // ng
    rows, head_count = queries.shape[:2]
    head_width = head_count * value_up.shape[2]
    block = out_proj.shape[1]
    width, units = 2 * block, down.shape[0]
    vmem, anywhere = pl.BlockSpec(memory_space=pltpu.VMEM), pl.BlockSpec(memory_space=pl.ANY)
    smem, dma = pl.BlockSpec(memory_space=pltpu.SMEM), pltpu.SemaphoreType.DMA
    return pl.pallas_call(
        functools.partial(layer_kernel, ng, nep),
        out_shape=jax.ShapeDtypeStruct((rows, nep * block), BF),
        in_specs=[smem, vmem, vmem, smem, smem, vmem] + [anywhere] * 5,
        out_specs=vmem,
        scratch_shapes=[
            pltpu.VMEM(cache.shape, BF),
            pltpu.VMEM(value_up.shape, BF),
            pltpu.VMEM(out_proj.shape, BF),
            pltpu.VMEM((ng, gate_up.shape[0], 2, 128), BF),
            pltpu.VMEM((gate_up.shape[0], ng * 256), BF),
            pltpu.VMEM((ng, units, width), BF),
            pltpu.VMEM((nep, rows, head_width), BF),
            pltpu.VMEM((owners, rows, block), BF),
            pltpu.VMEM((nep, rows, 128), F32),
            pltpu.VMEM((2, ng, rows, block), F32),
            pltpu.VMEM((2, ng, rows, block), BF),
            pltpu.VMEM((2, ng, rows, block), BF),
            pltpu.VMEM((2, nz, rows, block), BF),
            pltpu.VMEM((2, rows, 128), F32),
            pltpu.VMEM((2, 2, ng, rows, 128), F32),
            pltpu.VMEM((2, 2, ng, rows, block), BF),
            pltpu.VMEM((2, ng, nz * rows, 2 * units), BF),
            pltpu.VMEM((2, ng, nz * rows, 2 * units), BF),
            pltpu.VMEM((2, ng, nz * rows, units), BF),
            pltpu.VMEM((2, 2, nz, rows, block), BF),
            pltpu.VMEM((2, nz, rows, block), BF),
            pltpu.VMEM((2, nz, rows, block), BF),
            pltpu.VMEM((2, nz, rows, block), BF),
            pltpu.VMEM((2, ng, rows, block), BF),
            dma((8 + ng,)),
            dma((128,)),
            dma((nep,)),
            dma((owners,)),
            dma((nep,)),
            dma((2, ng)),
            dma((2, nz)),
            dma((2, 2, ng)),
            dma((2, 2, ng)),
            dma((2, ng)),
            dma((ng,)),
            dma((2, ng)),
            dma((2,)),
            dma((2, nz)),
            dma((2, ng)),
        ],
        compiler_params=pltpu.CompilerParams(
            collective_id=0, has_side_effects=True, vmem_limit_bytes=52 * 1024 * 1024
        ),
    )(lengths, queries, hidden, ids, gates, gain, cache, value_up, out_proj, gate_up, down)


def local_dense(
    hidden_in,
    queries,
    latent_cache,
    cache_lengths,
    expert_ids,
    gate_values,
    norm_gain,
    value_up,
    out_proj,
    gate_up,
    down_proj,
):
    nep = lax.axis_size("ep")
    micro, row_local, feature_count = hidden_in.shape
    rows = micro * row_local

    def merged(array):
        return array.reshape((rows,) + array.shape[2:])

    result = fused_layer(
        cache_lengths,
        merged(queries),
        merged(hidden_in),
        jnp.swapaxes(expert_ids, 1, 2),
        jnp.swapaxes(gate_values, 1, 2),
        norm_gain.reshape(nep, 1, feature_count // nep),
        jnp.swapaxes(merged(latent_cache), 1, 2),
        value_up,
        out_proj,
        gate_up[0],
        down_proj[0],
    )
    return result.reshape(hidden_in.shape)


def layer(*args):
    hidden_in, expert_ids, down_proj = args[0], args[4], args[10]
    ng, nep = lax.axis_size("group"), lax.axis_size("ep")
    micro, row_local, feature_count = hidden_in.shape
    dense = (
        2 * expert_ids.shape[2] == nep
        and nep == 2 * ng
        and feature_count % (nep * 128) == 0
        and micro * row_local == 16
        and down_proj.shape[1] == 128
        and ng % 2 == 0
    )
    return local_dense(*args) if dense else local(*args)


def solution(mesh):
    return jax.shard_map(
        layer,
        mesh=mesh,
        in_specs=(
            P(None, "ep", None),
            P(None, "ep", "group", None),
            P(None, "ep", None, None),
            P(None, "ep"),
            P(None, "ep", None),
            P(None, "ep", None),
            P(),
            P("group", None, None),
            P("group", "ep"),
            P("ep", "group", None, None),
            P("ep", "group", None),
        ),
        out_specs=P(None, "ep", None),
        check_vma=False,
    )
```

```python
import functools
import math

import jax
import jax.numpy as jnp
from jax import lax
from jax.experimental import pallas as pl
from jax.experimental.pallas import tpu as pltpu
from jax.sharding import PartitionSpec as P

ROPE = 64
NOPE = 128


def attend(queries, cache, lengths, value_up):
    row_count, head_count, key_width = queries.shape
    latent_width = value_up.shape[1]
    score_scale = 1.0 / math.sqrt(NOPE + ROPE)
    scores = (
        jnp.einsum("rhk,rlk->rhl", queries, cache, preferred_element_type=jnp.float32) * score_scale
    )
    in_range = jnp.arange(cache.shape[1], dtype=jnp.int32)[None, None, :] < lengths[:, None, None]
    masked = jnp.where(in_range, scores, -1e30)
    peak_score = jnp.max(masked, axis=2, keepdims=True)
    exponent = jnp.where(in_range, jnp.exp(masked - peak_score), 0.0)
    weights = (exponent / jnp.sum(exponent, axis=2, keepdims=True)).astype(jnp.bfloat16)
    latent = jnp.einsum(
        "rhl,rlc->rhc", weights, cache[:, :, :latent_width], preferred_element_type=jnp.float32
    ).astype(jnp.bfloat16)
    head_out = jnp.einsum(
        "rhc,hcv->rhv", latent, value_up, preferred_element_type=jnp.float32
    ).astype(jnp.bfloat16)
    return head_out.reshape(row_count, head_count * value_up.shape[2])


def rms_scale(residual, norm_gain):
    mean_square = jnp.mean(residual * residual, axis=1, keepdims=True)
    return (residual * lax.rsqrt(mean_square + 1e-06) * norm_gain[None, :]).astype(jnp.bfloat16)


def routing_tables(expert_ids, gate_values, expert_count, capacity):
    row_count, top_count = expert_ids.shape
    onehot = (
        expert_ids[:, :, None] == jnp.arange(expert_count, dtype=jnp.int32)[None, None, :]
    ).astype(jnp.int32)
    flat_hot = onehot.reshape(row_count * top_count, expert_count)
    before = jnp.cumsum(flat_hot, axis=0) - flat_hot
    slot_index = jnp.sum(before * flat_hot, axis=1).reshape(row_count, top_count)
    slot_hot = (
        slot_index[:, :, None] == jnp.arange(capacity, dtype=jnp.int32)[None, None, :]
    ).astype(jnp.float32)
    chosen = onehot.astype(jnp.float32)
    select = jnp.einsum("rke,rkc->ecr", chosen, slot_hot, precision=lax.Precision.HIGHEST)
    weighted = jnp.einsum(
        "rke,rkc,rk->ecr", chosen, slot_hot, gate_values, precision=lax.Precision.HIGHEST
    )
    return (select.astype(jnp.bfloat16), weighted)


def pack_rows(select, features):
    packed = jnp.einsum("ecr,rd->ecd", select, features, preferred_element_type=jnp.float32).astype(
        jnp.bfloat16
    )
    return jnp.repeat(packed, 2, axis=0)


def local(
    hidden_in,
    queries,
    latent_cache,
    cache_lengths,
    expert_ids,
    gate_values,
    norm_gain,
    value_up,
    out_proj,
    gate_up,
    down_proj,
):
    feature_count = hidden_in.shape[2]
    expert_count = lax.axis_size("ep") // 2
    row_local = hidden_in.shape[1]
    top_count = expert_ids.shape[2]
    capacity = min(row_local, 2 * row_local * top_count // expert_count)
    down_local = down_proj[0]
    moved = lax.all_to_all(gate_up, "group", split_axis=3, concat_axis=1, tiled=True)
    local_gate_up = moved[0].reshape(feature_count, -1)
    results = []
    for micro in range(hidden_in.shape[0]):
        head_values = attend(queries[micro], latent_cache[micro], cache_lengths[micro], value_up)
        spread = jnp.dot(
            lax.all_gather(head_values, "ep", axis=0, tiled=True),
            out_proj,
            preferred_element_type=jnp.float32,
        )
        own_rows = lax.all_to_all(spread, "ep", split_axis=0, concat_axis=1, tiled=True)
        attended = lax.psum(own_rows, "group")
        residual = hidden_in[micro].astype(jnp.float32) + attended
        normed = rms_scale(residual, norm_gain)
        select, weighted = routing_tables(
            expert_ids[micro], gate_values[micro], expert_count, capacity
        )
        outgoing = pack_rows(select, normed)
        received = lax.all_to_all(outgoing, "ep", split_axis=0, concat_axis=0, tiled=True)
        rollout_senders, rollout_item_count, width_in = received.shape
        rollout_pre_act = jnp.dot(
            received.reshape(rollout_senders * rollout_item_count, width_in),
            local_gate_up,
            preferred_element_type=jnp.float32,
        )
        pre_act = rollout_pre_act.reshape(rollout_senders * rollout_item_count, 2, -1)
        activation = (jax.nn.silu(pre_act[:, 0]) * pre_act[:, 1]).astype(jnp.bfloat16)
        block_part = jnp.dot(activation, down_local, preferred_element_type=jnp.float32).reshape(
            rollout_senders, rollout_item_count, feature_count
        )
        gathered = lax.all_to_all(
            block_part.astype(jnp.bfloat16), "ep", split_axis=0, concat_axis=0, tiled=True
        ).astype(block_part.dtype)
        gathered = gathered.reshape(expert_count, 2, capacity, -1)
        expert_mix = jnp.einsum("ecr,ehcd->rd", weighted, gathered, precision=lax.Precision.HIGHEST)
        expert_total = lax.psum(expert_mix.astype(jnp.bfloat16), "group").astype(jnp.float32)
        results.append((residual + expert_total).astype(jnp.bfloat16))
    return jnp.stack(results)


MESH = pl.DeviceIdType.MESH
BF = jnp.bfloat16
F32 = jnp.float32


def attend_rows(len_ref, q_ref, cache, cache_loads, latent_width):
    rows, head_count = q_ref.shape[:2]
    length = cache.shape[2]
    chunk = rows // len(cache_loads)
    score_scale = 1.0 / math.sqrt(NOPE + ROPE)
    position = lax.broadcasted_iota(jnp.int32, (head_count, length), 1)
    masked = []
    for r in range(rows):
        if r % chunk == 0:
            cache_loads[r // chunk].wait()
        scores = jnp.dot(q_ref[r], cache[r], preferred_element_type=F32) * score_scale
        in_range = position < len_ref[r // len_ref.shape[1], r % len_ref.shape[1]]
        masked.append(jnp.where(in_range, scores, -1e30))
    masked = jnp.concatenate(masked, axis=0)
    exponent = jnp.exp(masked - jnp.max(masked, axis=1, keepdims=True))
    weights = exponent / jnp.sum(exponent, axis=1, keepdims=True)
    turned = jnp.transpose(weights).astype(BF)
    column = lax.broadcasted_iota(jnp.int32, (latent_width, rows * head_count), 1)
    latents = jnp.zeros((latent_width, rows * head_count), F32)
    for r in range(rows):
        mixed = jnp.dot(cache[r, :latent_width, :], turned, preferred_element_type=F32)
        latents = jnp.where(column // head_count == r, mixed, latents)
    return latents.astype(BF)


def layer_kernel(
    ng,
    nep,
    len_ref,
    q_hbm,
    hid_hbm,
    id_ref,
    gate_ref,
    gain_hbm,
    cache_hbm,
    vu_hbm,
    wo_hbm,
    gu_hbm,
    dn_hbm,
    out_ref,
    q_ref,
    gain_ref,
    cache,
    vu,
    wo,
    gu,
    gate_up,
    dn,
    heads,
    hid_blk,
    coefs,
    s_own,
    s_send,
    s_rx,
    ag,
    ssq_own,
    ssq_rx,
    res,
    pre_send,
    pre_rx,
    act,
    part,
    sib_rx,
    chip_sum,
    z_rx,
    fin,
    load_sem,
    send_sem,
    heads_sem,
    hid_sem,
    coef_sem,
    s_sem,
    ag_sem,
    ssq_sem,
    res_sem,
    pre_sem,
    dn_sem,
    act_sem,
    sib_sem,
    z_sem,
    fin_sem,
):
    g = lax.axis_index("group")
    j = lax.axis_index("ep")
    nz = nep // 2
    z = j // 2
    c = j % 2
    other = 1 - c
    sibling = (g, z * 2 + other)
    rows, head_count = q_ref.shape[:2]
    block = wo.shape[1]
    owners = nep // ng
    units = dn.shape[1]
    slice_width = 2 * block

    chunk = rows // 2
    cache_loads = [
        pltpu.make_async_copy(
            cache_hbm.at[pl.ds(i * chunk, chunk)], cache.at[pl.ds(i * chunk, chunk)], load_sem.at[i]
        )
        for i in range(2)
    ]
    vu_load = pltpu.make_async_copy(vu_hbm, vu, load_sem.at[4])
    wo_load = pltpu.make_async_copy(wo_hbm, wo, load_sem.at[5])
    gu_loads = [
        pltpu.make_async_copy(
            gu_hbm.at[:, :, pl.ds(s * 128, 128)], gu.at[s], load_sem.at[8 + s]
        )
        for s in range(ng)
    ]
    own_slice = pl.ds(pl.multiple_of(g * slice_width, 128), slice_width)
    dn_load = pltpu.make_async_copy(dn_hbm.at[:, own_slice], dn.at[g], load_sem.at[7])
    q_load = pltpu.make_async_copy(q_hbm, q_ref, load_sem.at[8 + ng])
    gain_load = pltpu.make_async_copy(gain_hbm, gain_ref, load_sem.at[9 + ng])
    for load in [q_load] + cache_loads + [vu_load, gain_load, wo_load, dn_load] + gu_loads:
        load.start()

    barrier = pltpu.get_barrier_semaphore()
    ep_peers = [(g, (j + d) % nep) for d in range(1, nep)]
    g_peers = [((g + d) % ng, j) for d in range(1, ng)]
    for peer in ep_peers + g_peers:
        pl.semaphore_signal(barrier, inc=1, device_id=peer, device_id_type=MESH)
    pl.semaphore_wait(barrier, len(ep_peers) + len(g_peers))

    sends = []

    def remote(src, dst, recv, peer, index):
        return pltpu.make_async_remote_copy(
            src_ref=src,
            dst_ref=dst,
            send_sem=send_sem.at[index],
            recv_sem=recv,
            device_id=peer,
            device_id_type=MESH,
        )

    def send(src, dst, recv, peer):
        copy = remote(src, dst, recv, peer, len(sends))
        copy.start()
        sends.append(copy)

    def send_if(wanted, src, dst, recv, peer):
        copy = remote(src, dst, recv, peer, len(sends))

        @pl.when(wanted)
        def _():
            copy.start()

        sends.append((wanted, copy))

    def arrived(dst, recv):
        remote(dst, dst, recv, sibling, 0).wait_recv()

    lane = lax.broadcasted_iota(jnp.int32, (1, 128), 1)
    micro, top_count, row_local = id_ref.shape
    for r in range(rows):
        row = jnp.zeros((1, 128), F32)
        for k in range(top_count):
            m, i = r // row_local, r % row_local
            row = row + jnp.where(lane == id_ref[m, k, i], gate_ref[m, k, i], 0.0)
        coefs[j, r : r + 1, :] = row
    for peer in ep_peers:
        send(coefs.at[j], coefs.at[j], coef_sem.at[j], peer)

    is_source = j // owners == g
    hid_sends = []
    for k, peer in enumerate(ep_peers):
        start = pl.multiple_of(peer[1] * block, 128)
        hid_sends.append(
            remote(
                hid_hbm.at[:, pl.ds(start, block)],
                hid_blk.at[j % owners],
                hid_sem.at[j % owners],
                peer,
                send_sem.shape[0] - nep + k,
            )
        )

    hid_load = pltpu.make_async_copy(
        hid_hbm.at[:, pl.ds(pl.multiple_of(j * block, 128), block)],
        hid_blk.at[j % owners],
        load_sem.at[2],
    )

    @pl.when(is_source)
    def _():
        for copy in hid_sends:
            copy.start()
        hid_load.start()
        hid_load.wait()

    for peer in g_peers:
        start = pl.multiple_of(peer[0] * slice_width, 128)
        send(dn_hbm.at[:, pl.ds(start, slice_width)], dn.at[g], dn_sem.at[g], peer)

    q_load.wait()
    latents = attend_rows(len_ref, q_ref, cache, cache_loads, vu.shape[1])
    vu_load.wait()
    count = rows * head_count
    to = lax.broadcasted_iota(jnp.int32, (count, count), 0)
    source = lax.broadcasted_iota(jnp.int32, (count, count), 1)
    swap = jnp.where(source == to % rows * head_count + to // rows, 1.0, 0.0).astype(BF)
    by_head = lax.dot_general(
        swap, latents, (((1,), (1,)), ((), ())), preferred_element_type=F32
    ).astype(BF)
    value_width = vu.shape[2]
    for h in range(head_count):
        heads[j, :, h * value_width : (h + 1) * value_width] = jnp.dot(
            by_head[h * rows : (h + 1) * rows], vu[h], preferred_element_type=F32
        ).astype(BF)

    for d in range(1, nz):
        send(heads.at[j], heads.at[j], heads_sem.at[j], (g, (z + d) % nz * 2 + c))
    send(heads.at[j], heads.at[j], heads_sem.at[j], sibling)
    for load in gu_loads:
        load.wait()
    to = lax.broadcasted_iota(jnp.int32, (256, 256), 0)
    source = lax.broadcasted_iota(jnp.int32, (256, 256), 1)
    wanted = jnp.where(to < 128, 2 * to, 2 * (to - 128) + 1)
    order = jnp.where(source == wanted, 1.0, 0.0).astype(BF)
    mixed = gu.reshape(ng, 2 * gu.shape[1], 128)
    for t in range(gu.shape[1] // 128):
        lines = jnp.concatenate([mixed[s, t * 256 : (t + 1) * 256, :] for s in range(ng)], axis=1)
        sorted_lines = jnp.dot(order, lines, preferred_element_type=F32).astype(BF)
        for s in range(ng):
            for i in range(2):
                gate_up[t * 128 : (t + 1) * 128, s * 256 + i * 128 : s * 256 + (i + 1) * 128] = (
                    sorted_lines[i * 128 : (i + 1) * 128, s * 128 : (s + 1) * 128]
                )

    for d in range(1, nz):
        slot = (z + d) % nz * 2 + c
        arrived(heads.at[slot], heads_sem.at[slot])
        send(heads.at[slot], heads.at[slot], heads_sem.at[slot], sibling)
    count = nz * rows

    def project(h):
        @pl.when(other == h)
        def _():
            for d in range(nz):
                slot = (z + d) % nz * 2 + other
                arrived(heads.at[slot], heads_sem.at[slot])

        rows_in = jnp.concatenate([heads[2 * i + h] for i in range(nz)], axis=0)
        spread = jnp.dot(rows_in, wo[...], preferred_element_type=F32)
        s_own[h] = spread.reshape(ng, rows, block)
        s_send[h] = spread.astype(BF).reshape(ng, rows, block)
        for peer in g_peers:
            send(s_send.at[h, peer[0]], s_rx.at[h, g], s_sem.at[h, g], peer)

    def add_heads(h):
        @pl.when(g * 2 + h != j)
        def _():
            arrived(hid_blk.at[h], hid_sem.at[h])

        total = s_own[h, g] + hid_blk[h].astype(F32)
        for d in range(1, ng):
            slot = (g + d) % ng
            arrived(s_rx.at[h, slot], s_sem.at[h, slot])
            total = total + s_rx[h, slot].astype(F32)
        ag[h, z] = total.astype(BF)
        for d in range(1, nz):
            send(ag.at[h, z], ag.at[h, z], ag_sem.at[h, z], (g, (z + d) % nz * 2 + c))

    def spread_blocks(h):
        square = None
        for d in range(nz):
            slot = (z + d) % nz
            if d:
                arrived(ag.at[h, slot], ag_sem.at[h, slot])
            send_if(
                slot != g, ag.at[h, slot], res.at[h, c, g], res_sem.at[h, c, g], (slot, j)
            )

            @pl.when(slot == g)
            def _(slot=slot):
                res[h, c, g] = ag[h, slot]

            value = ag[h, slot].astype(F32)
            term = jnp.sum(value * value, axis=1, keepdims=True)
            square = term if square is None else square + term
        ssq_own[h] = jnp.broadcast_to(square, ssq_own.shape[1:])
        ssq_rx[h, c, g] = ssq_own[h]
        for peer in g_peers:
            send(ssq_own.at[h], ssq_rx.at[h, c, g], ssq_sem.at[h, c, g], peer)

    def share_blocks(h):
        for ref, sem in ((res, res_sem), (ssq_rx, ssq_sem)):
            for d in range(ng):
                slot = (g + d) % ng
                if d:
                    arrived(ref.at[h, c, slot], sem.at[h, c, slot])
                send(ref.at[h, c, slot], ref.at[h, c, slot], sem.at[h, c, slot], sibling)

    def pre_activate(h):
        for ref, sem in ((res, res_sem), (ssq_rx, ssq_sem)):
            for d in range(ng):
                slot = (g + d) % ng
                arrived(ref.at[h, other, slot], sem.at[h, other, slot])
        mean_square = (ssq_rx[h, 0] + ssq_rx[h, 1]).reshape(count, 128)[:, :1] / (nep * block)
        scale = lax.rsqrt(mean_square + 1e-06)
        pieces = []
        for b in range(2):
            rows_in = res[h, b].reshape(count, block).astype(F32)
            pieces.append((rows_in * scale * gain_ref[2 * g + b]).astype(BF))
        pre = jnp.dot(
            jnp.concatenate(pieces, axis=1), gate_up[...], preferred_element_type=F32
        ).astype(BF)
        for s in range(ng):
            pre_send[h, s] = pre[:, s * 2 * units : (s + 1) * 2 * units]
        for peer in g_peers:
            send(pre_send.at[h, peer[0]], pre_rx.at[h, g], pre_sem.at[h, g], peer)

    def activate(h):
        pre_sum = pre_send[h, g].astype(F32)
        for d in range(1, ng):
            slot = (g + d) % ng
            arrived(pre_rx.at[h, slot], pre_sem.at[h, slot])
            pre_sum = pre_sum + pre_rx[h, slot].astype(F32)
        act[h, g] = (jax.nn.silu(pre_sum[:, :units]) * pre_sum[:, units:]).astype(BF)
        for peer in g_peers:
            send(act.at[h, g], act.at[h, g], act_sem.at[h, g], peer)

    def project_down(h):
        for d in range(1, ng):
            slot = (g + d) % ng
            arrived(act.at[h, slot], act_sem.at[h, slot])
        activation = jnp.concatenate([act[h, s] for s in range(ng)], axis=1)
        lane = lax.broadcasted_iota(jnp.int32, (count, 128), 1)
        gates = jnp.concatenate([coefs[2 * i + h] for i in range(nz)], axis=0)
        factor = jnp.sum(jnp.where(lane == z, gates, 0.0), axis=1, keepdims=True)
        for b in range(2):
            columns = dn[:, :, b * block : (b + 1) * block].reshape(ng * units, block)
            piece = jnp.dot(activation, columns, preferred_element_type=F32) * factor
            part[h, b] = piece.astype(BF).reshape(nz, rows, block)
            send_if(c != h, part.at[h, b], sib_rx.at[b], sib_sem.at[b], sibling)

    def add_cores(h):
        @pl.when(c == h)
        def _():
            for b in range(2):
                arrived(sib_rx.at[b], sib_sem.at[b])
                chip_sum[b] = (part[h, b].astype(F32) + sib_rx[b].astype(F32)).astype(BF)
                for copy in z_sends[b]:
                    copy.start()

    wo_load.wait()
    gain_load.wait()
    for h in range(2):
        project(h)
    for h in range(2):
        add_heads(h)
    for h in range(2):
        spread_blocks(h)
    for h in range(2):
        share_blocks(h)
    for h in range(2):
        pre_activate(h)
    for h in range(2):
        activate(h)
    for peer in ep_peers:
        arrived(coefs.at[peer[1]], coef_sem.at[peer[1]])
    dn_load.wait()
    for d in range(1, ng):
        slot = (g + d) % ng
        arrived(dn.at[slot], dn_sem.at[slot])
    z_sends = []
    for b in range(2):
        z_sends.append([])
        for d in range(1, nz):
            pz = (z + d) % nz
            copy = remote(
                chip_sum.at[b, pz], z_rx.at[b, z], z_sem.at[b, z], (g, pz * 2 + c), len(sends)
            )
            z_sends[b].append(copy)
            sends.append(copy)
    for h in range(2):
        project_down(h)
        add_cores(h)
    for b in range(2):
        own = chip_sum[b, z].astype(F32)
        for d in range(1, nz):
            slot = (z + d) % nz
            arrived(z_rx.at[b, slot], z_sem.at[b, slot])
            own = own + z_rx[b, slot].astype(F32)
        fin[b, g] = (res[c, b, z].astype(F32) + own).astype(BF)
        for peer in g_peers:
            send(fin.at[b, g], fin.at[b, g], fin_sem.at[b, g], peer)
    for b in range(2):
        for d in range(1, ng):
            slot = (g + d) % ng
            arrived(fin.at[b, slot], fin_sem.at[b, slot])
    for s in range(ng):
        for b in range(2):
            start = (2 * s + b) * block
            out_ref[:, start : start + block] = fin[b, s]

    for copy in sends:
        if isinstance(copy, tuple):

            @pl.when(copy[0])
            def _(copy=copy):
                copy[1].wait_send()

        else:
            copy.wait_send()

    @pl.when(is_source)
    def _():
        for copy in hid_sends:
            copy.wait_send()


def fused_layer(
    lengths, queries, hidden, ids, gates, gain, cache, value_up, out_proj, gate_up, down
):
    ng, nep = lax.axis_size("group"), lax.axis_size("ep")
    nz, owners = nep // 2, nep // ng
    rows, head_count = queries.shape[:2]
    head_width = head_count * value_up.shape[2]
    block = out_proj.shape[1]
    width, units = 2 * block, down.shape[0]
    vmem, anywhere = pl.BlockSpec(memory_space=pltpu.VMEM), pl.BlockSpec(memory_space=pl.ANY)
    smem, dma = pl.BlockSpec(memory_space=pltpu.SMEM), pltpu.SemaphoreType.DMA
    return pl.pallas_call(
        functools.partial(layer_kernel, ng, nep),
        out_shape=jax.ShapeDtypeStruct((rows, nep * block), BF),
        in_specs=[smem, anywhere, anywhere, smem, smem] + [anywhere] * 6,
        out_specs=vmem,
        scratch_shapes=[
            pltpu.VMEM(queries.shape, BF),
            pltpu.VMEM(gain.shape, F32),
            pltpu.VMEM(cache.shape, BF),
            pltpu.VMEM(value_up.shape, BF),
            pltpu.VMEM(out_proj.shape, BF),
            pltpu.VMEM((ng, gate_up.shape[0], 2, 128), BF),
            pltpu.VMEM((gate_up.shape[0], ng * 256), BF),
            pltpu.VMEM((ng, units, width), BF),
            pltpu.VMEM((nep, rows, head_width), BF),
            pltpu.VMEM((owners, rows, block), BF),
            pltpu.VMEM((nep, rows, 128), F32),
            pltpu.VMEM((2, ng, rows, block), F32),
            pltpu.VMEM((2, ng, rows, block), BF),
            pltpu.VMEM((2, ng, rows, block), BF),
            pltpu.VMEM((2, nz, rows, block), BF),
            pltpu.VMEM((2, rows, 128), F32),
            pltpu.VMEM((2, 2, ng, rows, 128), F32),
            pltpu.VMEM((2, 2, ng, rows, block), BF),
            pltpu.VMEM((2, ng, nz * rows, 2 * units), BF),
            pltpu.VMEM((2, ng, nz * rows, 2 * units), BF),
            pltpu.VMEM((2, ng, nz * rows, units), BF),
            pltpu.VMEM((2, 2, nz, rows, block), BF),
            pltpu.VMEM((2, nz, rows, block), BF),
            pltpu.VMEM((2, nz, rows, block), BF),
            pltpu.VMEM((2, nz, rows, block), BF),
            pltpu.VMEM((2, ng, rows, block), BF),
            dma((10 + ng,)),
            dma((128,)),
            dma((nep,)),
            dma((owners,)),
            dma((nep,)),
            dma((2, ng)),
            dma((2, nz)),
            dma((2, 2, ng)),
            dma((2, 2, ng)),
            dma((2, ng)),
            dma((ng,)),
            dma((2, ng)),
            dma((2,)),
            dma((2, nz)),
            dma((2, ng)),
        ],
        compiler_params=pltpu.CompilerParams(
            collective_id=0, has_side_effects=True, vmem_limit_bytes=60 * 1024 * 1024
        ),
    )(lengths, queries, hidden, ids, gates, gain, cache, value_up, out_proj, gate_up, down)


def local_dense(
    hidden_in,
    queries,
    latent_cache,
    cache_lengths,
    expert_ids,
    gate_values,
    norm_gain,
    value_up,
    out_proj,
    gate_up,
    down_proj,
):
    nep = lax.axis_size("ep")
    micro, row_local, feature_count = hidden_in.shape
    rows = micro * row_local

    def merged(array):
        return array.reshape((rows,) + array.shape[2:])

    result = fused_layer(
        cache_lengths,
        merged(queries),
        merged(hidden_in),
        jnp.swapaxes(expert_ids, 1, 2),
        jnp.swapaxes(gate_values, 1, 2),
        norm_gain.reshape(nep, 1, feature_count // nep),
        jnp.swapaxes(merged(latent_cache), 1, 2),
        value_up,
        out_proj,
        gate_up[0],
        down_proj[0],
    )
    return result.reshape(hidden_in.shape)


def layer(*args):
    hidden_in, expert_ids, down_proj = args[0], args[4], args[10]
    ng, nep = lax.axis_size("group"), lax.axis_size("ep")
    micro, row_local, feature_count = hidden_in.shape
    dense = (
        2 * expert_ids.shape[2] == nep
        and nep == 2 * ng
        and feature_count % (nep * 128) == 0
        and micro * row_local == 16
        and down_proj.shape[1] == 128
        and ng % 2 == 0
    )
    return local_dense(*args) if dense else local(*args)


def solution(mesh):
    return jax.shard_map(
        layer,
        mesh=mesh,
        in_specs=(
            P(None, "ep", None),
            P(None, "ep", "group", None),
            P(None, "ep", None, None),
            P(None, "ep"),
            P(None, "ep", None),
            P(None, "ep", None),
            P(),
            P("group", None, None),
            P("group", "ep"),
            P("ep", "group", None, None),
            P("ep", "group", None),
        ),
        out_specs=P(None, "ep", None),
        check_vma=False,
    )
```

```python
import functools
import math

import jax
import jax.numpy as jnp
from jax import lax
from jax.experimental import pallas as pl
from jax.experimental.pallas import tpu as pltpu
from jax.sharding import PartitionSpec as P

ROPE = 64
NOPE = 128


def attend(queries, cache, lengths, value_up):
    row_count, head_count, key_width = queries.shape
    latent_width = value_up.shape[1]
    score_scale = 1.0 / math.sqrt(NOPE + ROPE)
    scores = (
        jnp.einsum("rhk,rlk->rhl", queries, cache, preferred_element_type=jnp.float32) * score_scale
    )
    in_range = jnp.arange(cache.shape[1], dtype=jnp.int32)[None, None, :] < lengths[:, None, None]
    masked = jnp.where(in_range, scores, -1e30)
    peak_score = jnp.max(masked, axis=2, keepdims=True)
    exponent = jnp.where(in_range, jnp.exp(masked - peak_score), 0.0)
    weights = (exponent / jnp.sum(exponent, axis=2, keepdims=True)).astype(jnp.bfloat16)
    latent = jnp.einsum(
        "rhl,rlc->rhc", weights, cache[:, :, :latent_width], preferred_element_type=jnp.float32
    ).astype(jnp.bfloat16)
    head_out = jnp.einsum(
        "rhc,hcv->rhv", latent, value_up, preferred_element_type=jnp.float32
    ).astype(jnp.bfloat16)
    return head_out.reshape(row_count, head_count * value_up.shape[2])


def rms_scale(residual, norm_gain):
    mean_square = jnp.mean(residual * residual, axis=1, keepdims=True)
    return (residual * lax.rsqrt(mean_square + 1e-06) * norm_gain[None, :]).astype(jnp.bfloat16)


def routing_tables(expert_ids, gate_values, expert_count, capacity):
    row_count, top_count = expert_ids.shape
    onehot = (
        expert_ids[:, :, None] == jnp.arange(expert_count, dtype=jnp.int32)[None, None, :]
    ).astype(jnp.int32)
    flat_hot = onehot.reshape(row_count * top_count, expert_count)
    before = jnp.cumsum(flat_hot, axis=0) - flat_hot
    slot_index = jnp.sum(before * flat_hot, axis=1).reshape(row_count, top_count)
    slot_hot = (
        slot_index[:, :, None] == jnp.arange(capacity, dtype=jnp.int32)[None, None, :]
    ).astype(jnp.float32)
    chosen = onehot.astype(jnp.float32)
    select = jnp.einsum("rke,rkc->ecr", chosen, slot_hot, precision=lax.Precision.HIGHEST)
    weighted = jnp.einsum(
        "rke,rkc,rk->ecr", chosen, slot_hot, gate_values, precision=lax.Precision.HIGHEST
    )
    return (select.astype(jnp.bfloat16), weighted)


def pack_rows(select, features):
    packed = jnp.einsum("ecr,rd->ecd", select, features, preferred_element_type=jnp.float32).astype(
        jnp.bfloat16
    )
    return jnp.repeat(packed, 2, axis=0)


def local(
    hidden_in,
    queries,
    latent_cache,
    cache_lengths,
    expert_ids,
    gate_values,
    norm_gain,
    value_up,
    out_proj,
    gate_up,
    down_proj,
):
    feature_count = hidden_in.shape[2]
    expert_count = lax.axis_size("ep") // 2
    row_local = hidden_in.shape[1]
    top_count = expert_ids.shape[2]
    capacity = min(row_local, 2 * row_local * top_count // expert_count)
    down_local = down_proj[0]
    moved = lax.all_to_all(gate_up, "group", split_axis=3, concat_axis=1, tiled=True)
    local_gate_up = moved[0].reshape(feature_count, -1)
    results = []
    for micro in range(hidden_in.shape[0]):
        head_values = attend(queries[micro], latent_cache[micro], cache_lengths[micro], value_up)
        spread = jnp.dot(
            lax.all_gather(head_values, "ep", axis=0, tiled=True),
            out_proj,
            preferred_element_type=jnp.float32,
        )
        own_rows = lax.all_to_all(spread, "ep", split_axis=0, concat_axis=1, tiled=True)
        attended = lax.psum(own_rows, "group")
        residual = hidden_in[micro].astype(jnp.float32) + attended
        normed = rms_scale(residual, norm_gain)
        select, weighted = routing_tables(
            expert_ids[micro], gate_values[micro], expert_count, capacity
        )
        outgoing = pack_rows(select, normed)
        received = lax.all_to_all(outgoing, "ep", split_axis=0, concat_axis=0, tiled=True)
        rollout_senders, rollout_item_count, width_in = received.shape
        rollout_pre_act = jnp.dot(
            received.reshape(rollout_senders * rollout_item_count, width_in),
            local_gate_up,
            preferred_element_type=jnp.float32,
        )
        pre_act = rollout_pre_act.reshape(rollout_senders * rollout_item_count, 2, -1)
        activation = (jax.nn.silu(pre_act[:, 0]) * pre_act[:, 1]).astype(jnp.bfloat16)
        block_part = jnp.dot(activation, down_local, preferred_element_type=jnp.float32).reshape(
            rollout_senders, rollout_item_count, feature_count
        )
        gathered = lax.all_to_all(
            block_part.astype(jnp.bfloat16), "ep", split_axis=0, concat_axis=0, tiled=True
        ).astype(block_part.dtype)
        gathered = gathered.reshape(expert_count, 2, capacity, -1)
        expert_mix = jnp.einsum("ecr,ehcd->rd", weighted, gathered, precision=lax.Precision.HIGHEST)
        expert_total = lax.psum(expert_mix.astype(jnp.bfloat16), "group").astype(jnp.float32)
        results.append((residual + expert_total).astype(jnp.bfloat16))
    return jnp.stack(results)


MESH = pl.DeviceIdType.MESH
BF = jnp.bfloat16
F32 = jnp.float32


def attend_rows(len_ref, q_ref, cache, cache_loads, latent_width):
    rows, head_count = q_ref.shape[:2]
    length = cache.shape[2]
    chunk = rows // len(cache_loads)
    score_scale = 1.0 / math.sqrt(NOPE + ROPE)
    position = lax.broadcasted_iota(jnp.int32, (head_count, length), 1)
    masked = []
    for r in range(rows):
        if r % chunk == 0:
            cache_loads[r // chunk].wait()
        scores = jnp.dot(q_ref[r], cache[r], preferred_element_type=F32) * score_scale
        in_range = position < len_ref[r // len_ref.shape[1], r % len_ref.shape[1]]
        masked.append(jnp.where(in_range, scores, -1e30))
    masked = jnp.concatenate(masked, axis=0)
    exponent = jnp.exp(masked - jnp.max(masked, axis=1, keepdims=True))
    weights = (exponent / jnp.sum(exponent, axis=1, keepdims=True)).astype(BF)
    latents = [
        lax.dot_general(
            weights[r * head_count : (r + 1) * head_count],
            cache[r, :latent_width, :],
            (((1,), (1,)), ((), ())),
            preferred_element_type=F32,
        ).astype(BF)
        for r in range(rows)
    ]
    return jnp.concatenate(latents, axis=0)


def layer_kernel(
    ng,
    nep,
    len_ref,
    q_hbm,
    hid_hbm,
    id_ref,
    gate_ref,
    gain_hbm,
    cache_hbm,
    vu_hbm,
    wo_hbm,
    gu_hbm,
    dn_hbm,
    out_ref,
    q_ref,
    gain_ref,
    cache,
    vu,
    wo,
    gu,
    gate_up,
    dn,
    heads,
    hid_blk,
    coefs,
    s_own,
    s_send,
    s_rx,
    ag,
    ssq_own,
    ssq_rx,
    res,
    pre_send,
    pre_rx,
    act,
    part,
    sib_rx,
    chip_sum,
    z_rx,
    fin,
    load_sem,
    send_sem,
    heads_sem,
    hid_sem,
    coef_sem,
    s_sem,
    ag_sem,
    ssq_sem,
    res_sem,
    pre_sem,
    dn_sem,
    act_sem,
    sib_sem,
    z_sem,
    fin_sem,
):
    g = lax.axis_index("group")
    j = lax.axis_index("ep")
    nz = nep // 2
    z = j // 2
    c = j % 2
    other = 1 - c
    sibling = (g, z * 2 + other)
    rows, head_count = q_ref.shape[:2]
    block = wo.shape[1]
    owners = nep // ng
    units = dn.shape[1]
    slice_width = 2 * block

    chunk = rows // 2
    cache_loads = [
        pltpu.make_async_copy(
            cache_hbm.at[pl.ds(i * chunk, chunk)], cache.at[pl.ds(i * chunk, chunk)], load_sem.at[i]
        )
        for i in range(2)
    ]
    vu_load = pltpu.make_async_copy(vu_hbm, vu, load_sem.at[4])
    wo_load = pltpu.make_async_copy(wo_hbm, wo, load_sem.at[5])
    gu_loads = [
        pltpu.make_async_copy(
            gu_hbm.at[:, :, pl.ds(s * 128, 128)], gu.at[s], load_sem.at[8 + s]
        )
        for s in range(ng)
    ]
    own_slice = pl.ds(pl.multiple_of(g * slice_width, 128), slice_width)
    dn_load = pltpu.make_async_copy(dn_hbm.at[:, own_slice], dn.at[g], load_sem.at[7])
    q_load = pltpu.make_async_copy(q_hbm, q_ref, load_sem.at[8 + ng])
    gain_load = pltpu.make_async_copy(gain_hbm, gain_ref, load_sem.at[9 + ng])
    for load in [q_load] + cache_loads + [vu_load, gain_load, wo_load, dn_load] + gu_loads:
        load.start()

    barrier = pltpu.get_barrier_semaphore()
    ep_peers = [(g, (j + d) % nep) for d in range(1, nep)]
    g_peers = [((g + d) % ng, j) for d in range(1, ng)]
    for peer in ep_peers + g_peers:
        pl.semaphore_signal(barrier, inc=1, device_id=peer, device_id_type=MESH)
    pl.semaphore_wait(barrier, len(ep_peers) + len(g_peers))

    sends = []

    def remote(src, dst, recv, peer, index):
        return pltpu.make_async_remote_copy(
            src_ref=src,
            dst_ref=dst,
            send_sem=send_sem.at[index],
            recv_sem=recv,
            device_id=peer,
            device_id_type=MESH,
        )

    def send(src, dst, recv, peer):
        copy = remote(src, dst, recv, peer, len(sends))
        copy.start()
        sends.append(copy)

    def send_if(wanted, src, dst, recv, peer):
        copy = remote(src, dst, recv, peer, len(sends))

        @pl.when(wanted)
        def _():
            copy.start()

        sends.append((wanted, copy))

    def arrived(dst, recv):
        remote(dst, dst, recv, sibling, 0).wait_recv()

    lane = lax.broadcasted_iota(jnp.int32, (1, 128), 1)
    micro, top_count, row_local = id_ref.shape
    for r in range(rows):
        row = jnp.zeros((1, 128), F32)
        for k in range(top_count):
            m, i = r // row_local, r % row_local
            row = row + jnp.where(lane == id_ref[m, k, i], gate_ref[m, k, i], 0.0)
        coefs[j, r : r + 1, :] = row
    for peer in ep_peers:
        send(coefs.at[j], coefs.at[j], coef_sem.at[j], peer)

    is_source = j // owners == g
    hid_sends = []
    for k, peer in enumerate(ep_peers):
        start = pl.multiple_of(peer[1] * block, 128)
        hid_sends.append(
            remote(
                hid_hbm.at[:, pl.ds(start, block)],
                hid_blk.at[j % owners],
                hid_sem.at[j % owners],
                peer,
                send_sem.shape[0] - nep + k,
            )
        )

    hid_load = pltpu.make_async_copy(
        hid_hbm.at[:, pl.ds(pl.multiple_of(j * block, 128), block)],
        hid_blk.at[j % owners],
        load_sem.at[2],
    )

    @pl.when(is_source)
    def _():
        for copy in hid_sends:
            copy.start()
        hid_load.start()
        hid_load.wait()

    for peer in g_peers:
        start = pl.multiple_of(peer[0] * slice_width, 128)
        send(dn_hbm.at[:, pl.ds(start, slice_width)], dn.at[g], dn_sem.at[g], peer)

    q_load.wait()
    latents = attend_rows(len_ref, q_ref, cache, cache_loads, vu.shape[1])
    vu_load.wait()
    count = rows * head_count
    to = lax.broadcasted_iota(jnp.int32, (count, count), 0)
    source = lax.broadcasted_iota(jnp.int32, (count, count), 1)
    swap = jnp.where(source == to % rows * head_count + to // rows, 1.0, 0.0).astype(BF)
    by_head = jnp.dot(swap, latents, preferred_element_type=F32).astype(BF)
    value_width = vu.shape[2]
    for h in range(head_count):
        heads[j, :, h * value_width : (h + 1) * value_width] = jnp.dot(
            by_head[h * rows : (h + 1) * rows], vu[h], preferred_element_type=F32
        ).astype(BF)

    for d in range(1, nz):
        send(heads.at[j], heads.at[j], heads_sem.at[j], (g, (z + d) % nz * 2 + c))
    send(heads.at[j], heads.at[j], heads_sem.at[j], sibling)
    for load in gu_loads:
        load.wait()
    to = lax.broadcasted_iota(jnp.int32, (256, 256), 0)
    source = lax.broadcasted_iota(jnp.int32, (256, 256), 1)
    wanted = jnp.where(to < 128, 2 * to, 2 * (to - 128) + 1)
    order = jnp.where(source == wanted, 1.0, 0.0).astype(BF)
    mixed = gu.reshape(ng, 2 * gu.shape[1], 128)
    for t in range(gu.shape[1] // 128):
        lines = jnp.concatenate([mixed[s, t * 256 : (t + 1) * 256, :] for s in range(ng)], axis=1)
        sorted_lines = jnp.dot(order, lines, preferred_element_type=F32).astype(BF)
        for s in range(ng):
            for i in range(2):
                gate_up[t * 128 : (t + 1) * 128, s * 256 + i * 128 : s * 256 + (i + 1) * 128] = (
                    sorted_lines[i * 128 : (i + 1) * 128, s * 128 : (s + 1) * 128]
                )

    for d in range(1, nz):
        slot = (z + d) % nz * 2 + c
        arrived(heads.at[slot], heads_sem.at[slot])
        send(heads.at[slot], heads.at[slot], heads_sem.at[slot], sibling)
    count = nz * rows

    def project(h):
        @pl.when(other == h)
        def _():
            for d in range(nz):
                slot = (z + d) % nz * 2 + other
                arrived(heads.at[slot], heads_sem.at[slot])

        rows_in = jnp.concatenate([heads[2 * i + h] for i in range(nz)], axis=0)
        spread = jnp.dot(rows_in, wo[...], preferred_element_type=F32)
        s_own[h] = spread.reshape(ng, rows, block)
        s_send[h] = spread.astype(BF).reshape(ng, rows, block)
        for peer in g_peers:
            send(s_send.at[h, peer[0]], s_rx.at[h, g], s_sem.at[h, g], peer)

    def add_heads(h):
        @pl.when(g * 2 + h != j)
        def _():
            arrived(hid_blk.at[h], hid_sem.at[h])

        total = s_own[h, g] + hid_blk[h].astype(F32)
        for d in range(1, ng):
            slot = (g + d) % ng
            arrived(s_rx.at[h, slot], s_sem.at[h, slot])
            total = total + s_rx[h, slot].astype(F32)
        ag[h, z] = total.astype(BF)
        for d in range(1, nz):
            send(ag.at[h, z], ag.at[h, z], ag_sem.at[h, z], (g, (z + d) % nz * 2 + c))

    def spread_blocks(h):
        square = None
        for d in range(nz):
            slot = (z + d) % nz
            if d:
                arrived(ag.at[h, slot], ag_sem.at[h, slot])
            send_if(
                slot != g, ag.at[h, slot], res.at[h, c, g], res_sem.at[h, c, g], (slot, j)
            )

            @pl.when(slot == g)
            def _(slot=slot):
                res[h, c, g] = ag[h, slot]

            value = ag[h, slot].astype(F32)
            term = jnp.sum(value * value, axis=1, keepdims=True)
            square = term if square is None else square + term
        ssq_own[h] = jnp.broadcast_to(square, ssq_own.shape[1:])
        ssq_rx[h, c, g] = ssq_own[h]
        for peer in g_peers:
            send(ssq_own.at[h], ssq_rx.at[h, c, g], ssq_sem.at[h, c, g], peer)

    def share_blocks(h):
        for ref, sem in ((res, res_sem), (ssq_rx, ssq_sem)):
            for d in range(ng):
                slot = (g + d) % ng
                if d:
                    arrived(ref.at[h, c, slot], sem.at[h, c, slot])
                send(ref.at[h, c, slot], ref.at[h, c, slot], sem.at[h, c, slot], sibling)

    def pre_activate(h):
        for ref, sem in ((res, res_sem), (ssq_rx, ssq_sem)):
            for d in range(ng):
                slot = (g + d) % ng
                arrived(ref.at[h, other, slot], sem.at[h, other, slot])
        mean_square = (ssq_rx[h, 0] + ssq_rx[h, 1]).reshape(count, 128)[:, :1] / (nep * block)
        scale = lax.rsqrt(mean_square + 1e-06)
        pieces = []
        for b in range(2):
            rows_in = res[h, b].reshape(count, block).astype(F32)
            pieces.append((rows_in * scale * gain_ref[2 * g + b]).astype(BF))
        pre = jnp.dot(
            jnp.concatenate(pieces, axis=1), gate_up[...], preferred_element_type=F32
        ).astype(BF)
        for s in range(ng):
            pre_send[h, s] = pre[:, s * 2 * units : (s + 1) * 2 * units]
        for peer in g_peers:
            send(pre_send.at[h, peer[0]], pre_rx.at[h, g], pre_sem.at[h, g], peer)

    def activate(h):
        pre_sum = pre_send[h, g].astype(F32)
        for d in range(1, ng):
            slot = (g + d) % ng
            arrived(pre_rx.at[h, slot], pre_sem.at[h, slot])
            pre_sum = pre_sum + pre_rx[h, slot].astype(F32)
        act[h, g] = (jax.nn.silu(pre_sum[:, :units]) * pre_sum[:, units:]).astype(BF)
        for peer in g_peers:
            send(act.at[h, g], act.at[h, g], act_sem.at[h, g], peer)

    def project_down(h):
        for d in range(1, ng):
            slot = (g + d) % ng
            arrived(act.at[h, slot], act_sem.at[h, slot])
        activation = jnp.concatenate([act[h, s] for s in range(ng)], axis=1)
        lane = lax.broadcasted_iota(jnp.int32, (count, 128), 1)
        gates = jnp.concatenate([coefs[2 * i + h] for i in range(nz)], axis=0)
        factor = jnp.sum(jnp.where(lane == z, gates, 0.0), axis=1, keepdims=True)
        for b in range(2):
            columns = dn[:, :, b * block : (b + 1) * block].reshape(ng * units, block)
            piece = jnp.dot(activation, columns, preferred_element_type=F32) * factor
            part[h, b] = piece.astype(BF).reshape(nz, rows, block)
            send_if(c != h, part.at[h, b], sib_rx.at[b], sib_sem.at[b], sibling)

    def add_cores(h):
        @pl.when(c == h)
        def _():
            for b in range(2):
                arrived(sib_rx.at[b], sib_sem.at[b])
                chip_sum[b] = (part[h, b].astype(F32) + sib_rx[b].astype(F32)).astype(BF)
                for copy in z_sends[b]:
                    copy.start()

    wo_load.wait()
    gain_load.wait()
    for h in range(2):
        project(h)
    for h in range(2):
        add_heads(h)
    for h in range(2):
        spread_blocks(h)
    for h in range(2):
        share_blocks(h)
    for h in range(2):
        pre_activate(h)
    for h in range(2):
        activate(h)
    for peer in ep_peers:
        arrived(coefs.at[peer[1]], coef_sem.at[peer[1]])
    dn_load.wait()
    for d in range(1, ng):
        slot = (g + d) % ng
        arrived(dn.at[slot], dn_sem.at[slot])
    z_sends = []
    for b in range(2):
        z_sends.append([])
        for d in range(1, nz):
            pz = (z + d) % nz
            copy = remote(
                chip_sum.at[b, pz], z_rx.at[b, z], z_sem.at[b, z], (g, pz * 2 + c), len(sends)
            )
            z_sends[b].append(copy)
            sends.append(copy)
    for h in range(2):
        project_down(h)
        add_cores(h)
    for b in range(2):
        own = chip_sum[b, z].astype(F32)
        for d in range(1, nz):
            slot = (z + d) % nz
            arrived(z_rx.at[b, slot], z_sem.at[b, slot])
            own = own + z_rx[b, slot].astype(F32)
        fin[b, g] = (res[c, b, z].astype(F32) + own).astype(BF)
        for peer in g_peers:
            send(fin.at[b, g], fin.at[b, g], fin_sem.at[b, g], peer)
    for b in range(2):
        for d in range(1, ng):
            slot = (g + d) % ng
            arrived(fin.at[b, slot], fin_sem.at[b, slot])
    for s in range(ng):
        for b in range(2):
            start = (2 * s + b) * block
            out_ref[:, start : start + block] = fin[b, s]

    for copy in sends:
        if isinstance(copy, tuple):

            @pl.when(copy[0])
            def _(copy=copy):
                copy[1].wait_send()

        else:
            copy.wait_send()

    @pl.when(is_source)
    def _():
        for copy in hid_sends:
            copy.wait_send()


def fused_layer(
    lengths, queries, hidden, ids, gates, gain, cache, value_up, out_proj, gate_up, down
):
    ng, nep = lax.axis_size("group"), lax.axis_size("ep")
    nz, owners = nep // 2, nep // ng
    rows, head_count = queries.shape[:2]
    head_width = head_count * value_up.shape[2]
    block = out_proj.shape[1]
    width, units = 2 * block, down.shape[0]
    vmem, anywhere = pl.BlockSpec(memory_space=pltpu.VMEM), pl.BlockSpec(memory_space=pl.ANY)
    smem, dma = pl.BlockSpec(memory_space=pltpu.SMEM), pltpu.SemaphoreType.DMA
    return pl.pallas_call(
        functools.partial(layer_kernel, ng, nep),
        out_shape=jax.ShapeDtypeStruct((rows, nep * block), BF),
        in_specs=[smem, anywhere, anywhere, smem, smem] + [anywhere] * 6,
        out_specs=vmem,
        scratch_shapes=[
            pltpu.VMEM(queries.shape, BF),
            pltpu.VMEM(gain.shape, F32),
            pltpu.VMEM(cache.shape, BF),
            pltpu.VMEM(value_up.shape, BF),
            pltpu.VMEM(out_proj.shape, BF),
            pltpu.VMEM((ng, gate_up.shape[0], 2, 128), BF),
            pltpu.VMEM((gate_up.shape[0], ng * 256), BF),
            pltpu.VMEM((ng, units, width), BF),
            pltpu.VMEM((nep, rows, head_width), BF),
            pltpu.VMEM((owners, rows, block), BF),
            pltpu.VMEM((nep, rows, 128), F32),
            pltpu.VMEM((2, ng, rows, block), F32),
            pltpu.VMEM((2, ng, rows, block), BF),
            pltpu.VMEM((2, ng, rows, block), BF),
            pltpu.VMEM((2, nz, rows, block), BF),
            pltpu.VMEM((2, rows, 128), F32),
            pltpu.VMEM((2, 2, ng, rows, 128), F32),
            pltpu.VMEM((2, 2, ng, rows, block), BF),
            pltpu.VMEM((2, ng, nz * rows, 2 * units), BF),
            pltpu.VMEM((2, ng, nz * rows, 2 * units), BF),
            pltpu.VMEM((2, ng, nz * rows, units), BF),
            pltpu.VMEM((2, 2, nz, rows, block), BF),
            pltpu.VMEM((2, nz, rows, block), BF),
            pltpu.VMEM((2, nz, rows, block), BF),
            pltpu.VMEM((2, nz, rows, block), BF),
            pltpu.VMEM((2, ng, rows, block), BF),
            dma((10 + ng,)),
            dma((128,)),
            dma((nep,)),
            dma((owners,)),
            dma((nep,)),
            dma((2, ng)),
            dma((2, nz)),
            dma((2, 2, ng)),
            dma((2, 2, ng)),
            dma((2, ng)),
            dma((ng,)),
            dma((2, ng)),
            dma((2,)),
            dma((2, nz)),
            dma((2, ng)),
        ],
        compiler_params=pltpu.CompilerParams(
            collective_id=0, has_side_effects=True, vmem_limit_bytes=60 * 1024 * 1024
        ),
    )(lengths, queries, hidden, ids, gates, gain, cache, value_up, out_proj, gate_up, down)


def local_dense(
    hidden_in,
    queries,
    latent_cache,
    cache_lengths,
    expert_ids,
    gate_values,
    norm_gain,
    value_up,
    out_proj,
    gate_up,
    down_proj,
):
    nep = lax.axis_size("ep")
    micro, row_local, feature_count = hidden_in.shape
    rows = micro * row_local

    def merged(array):
        return array.reshape((rows,) + array.shape[2:])

    result = fused_layer(
        cache_lengths,
        merged(queries),
        merged(hidden_in),
        jnp.swapaxes(expert_ids, 1, 2),
        jnp.swapaxes(gate_values, 1, 2),
        norm_gain.reshape(nep, 1, feature_count // nep),
        jnp.swapaxes(merged(latent_cache), 1, 2),
        value_up,
        out_proj,
        gate_up[0],
        down_proj[0],
    )
    return result.reshape(hidden_in.shape)


def layer(*args):
    hidden_in, expert_ids, down_proj = args[0], args[4], args[10]
    ng, nep = lax.axis_size("group"), lax.axis_size("ep")
    micro, row_local, feature_count = hidden_in.shape
    dense = (
        2 * expert_ids.shape[2] == nep
        and nep == 2 * ng
        and feature_count % (nep * 128) == 0
        and micro * row_local == 16
        and down_proj.shape[1] == 128
        and ng % 2 == 0
    )
    return local_dense(*args) if dense else local(*args)


def solution(mesh):
    return jax.shard_map(
        layer,
        mesh=mesh,
        in_specs=(
            P(None, "ep", None),
            P(None, "ep", "group", None),
            P(None, "ep", None, None),
            P(None, "ep"),
            P(None, "ep", None),
            P(None, "ep", None),
            P(),
            P("group", None, None),
            P("group", "ep"),
            P("ep", "group", None, None),
            P("ep", "group", None),
        ),
        out_specs=P(None, "ep", None),
        check_vma=False,
    )
```
